256 devices in a mesh: seq: 8 (over y, core), ep: 32 (over x, z).
Axes of the slice: x: 4, y: 4, z: 8, core: 2. Of those that a mesh axis runs over, the one named last changes fastest.
Arguments:
- entering: bfloat16 [32, 32, 7168], P('ep', 'seq'), may hold values from -6 to 6
- moe_gain: float32 [7168], replicated, may hold values from 0.1 to 1.9
- expert_ids: int32 [32, 32, 8], P('ep'), may hold values from 0 to 31, all different within a row; in each aligned block of 4 rows (0 to 3, 4 to 7, ..., all dimensions but the last counted through in order) at most 2 rows name the same one
- gate_weights: float32 [32, 32, 8], P('ep'), may hold values from 0.05 to 0.5
- w_gate: bfloat16 [32, 7168, 2048], P('ep', None, 'seq'), may hold values from -0.0625 to 0.0625
- w_up: bfloat16 [32, 7168, 2048], P('ep', None, 'seq'), may hold values from -0.0625 to 0.0625
- w_down: bfloat16 [32, 2048, 7168], P('ep', 'seq'), may hold values from -0.125 to 0.125
- w_latent: bfloat16 [7168, 512], P('seq'), may hold values from -0.0625 to 0.0625
- w_rope: bfloat16 [64, 7168], P(None, 'seq'), may hold values from -0.0625 to 0.0625
- latent_gain: float32 [512], replicated, may hold values from 0.1 to 1.9
- prefix_len: int32 [32], P('ep'), may hold values from 128 to 1024, as said below
- cache_latent: bfloat16 [32, 1024, 512], P('ep', 'seq'), may hold values from -4 to 4
- cache_rope: bfloat16 [32, 64, 1024], P('ep', None, 'seq'), may hold values from -4 to 4
- query_latent: bfloat16 [32, 32, 65536], P('ep', 'seq'), may hold values from -7 to 7
- query_rope: bfloat16 [32, 32, 8192], P('ep', 'seq'), may hold values from -32 to 32
Outputs:
- layer_out: bfloat16 [32, 32, 7168], P('ep', None, 'seq')
- attention: bfloat16 [32, 32, 65536], P('ep', 'seq')
The draws below stay inside these ranges and needn't reach their ends.
Inputs may be any that keep to these rules, and one draw needn't show every extreme that they name: `expert_ids`: in each aligned block of 4 rows (one document's new tokens on one index of seq) no expert is named by more than 2 tokens, and in some blocks one is named by exactly 2. Each token names 8 different experts. `prefix_len`: some document has all 1024 positions cached.
All inputs are finite; a program needn't handle non-finite values.
Results may differ from the reference program's by a relative error of at most 0.018.
Values may be sent and summed in bfloat16 or wider, within the bound.
A program may use at most 128 MiB of HBM per device.

```python
import math
import jax
import jax.numpy as jnp
import numpy as np
from jax import lax

D = 7168
H = 128
LAT = 512
ROPE = 64
FF = 2048
TOP = 8
NEW_DEV = 4
EXPERTS = 32
DOCS = 32
NEW = 32
CACHE = 1024
FF_DEV = 256
CAP = 2
N_SEQ = 8


def draw_prefix_len(key, part):
    base = jax.random.fold_in(key, 51)
    values = jax.random.randint(base, (DOCS,), CACHE // 8, CACHE + 1)
    chosen = jax.random.randint(jax.random.fold_in(base, 1), (), 0, DOCS)
    return values.at[chosen].set(CACHE).astype(jnp.int32)


def draw_cache_rope(key, part):
    base = jax.random.fold_in(key, 31)
    values = jnp.clip(jax.random.normal(base, (DOCS, ROPE, CACHE), jnp.float32), -4.0, 4.0)
    return values.astype(jnp.bfloat16)


def draw_query_rope(key, part):
    base = jax.random.fold_in(key, 41)
    values = jnp.clip(0.6 * jax.random.normal(base, (DOCS, NEW, H, ROPE), jnp.float32), -4.0, 4.0)
    return values.reshape(DOCS, NEW, H * ROPE).astype(jnp.bfloat16)


def steps_of(rng, dims, shards, low, top_value):
    def one(dim, parts):
        heights = jax.random.uniform(jax.random.fold_in(jax.random.fold_in(rng, 6), dim), (parts,), jnp.float32, low / len(shards), top_value / len(shards))
        return jnp.repeat(jnp.exp(heights), dims[dim] // parts).reshape((-1,) + (1,) * (len(dims) - dim - 1))

    level = one(*shards[0])
    for cut in shards[1:]:
        level = level * one(*cut)
    return level


def deal_out(own_key, own, number, rows, number_of, top, reach, skew):
    ranking = jax.random.permutation(own_key, number_of)
    crowded, usual = load_shares(number_of, rows * top, reach, skew, True), load_shares(number_of, rows * top, reach, skew, False)
    places = jnp.arange(number_of)

    def named(sizes, rotation):
        used = int((sizes > 0).sum())
        fixed = max(1, used // 4)
        shifted = fixed + (places - fixed + rotation * (used - fixed)) % max(1, number_of - fixed)
        return jnp.zeros((number_of,), jnp.int32).at[ranking[jnp.where(places < fixed, places, shifted)]].set(jnp.asarray(sizes, jnp.int32))

    sizes = jnp.where(number % 4 == 0, named(crowded, number // 4), named(usual, number - number // 4 - 1))
    mixed = jax.random.permutation(jax.random.fold_in(own, 3), number_of)
    source_of, taker = mixed[0:number_of // 2 * 2:2], mixed[1:number_of // 2 * 2:2]
    margin = jnp.minimum(sizes[source_of] - 1, reach - sizes[taker]) // 2
    margin = jnp.where((source_of == ranking[0]) | (taker == ranking[0]) | (sizes[taker] == 0), 0, jnp.maximum(margin, 0))
    shifted = jax.random.randint(jax.random.fold_in(own, 4), (number_of // 2,), 0, 1 << 20) % (margin + 1)
    sizes = sizes.at[source_of].add(-shifted).at[taker].add(shifted)
    labels = jnp.searchsorted(jnp.cumsum(sizes), jnp.arange(rows * top), side="right").astype(jnp.int32)
    listing = labels.reshape(top, rows).T
    listing = listing[jax.random.permutation(jax.random.fold_in(own, 1), rows)]
    rotation = jax.random.randint(jax.random.fold_in(own, 2), (rows, 1), 0, top)
    return jnp.take_along_axis(listing, (jnp.arange(top)[None, :] + rotation) % top, axis=1)


def load_shares(count, total, reach, skew, full):
    loads = [(1 << 20) // math.isqrt(grade ** skew) + 1 for grade in range(1, count + 1)]
    largest = reach if full else min(reach, max(-(-total // count), total * loads[0] // sum(loads)))
    least = 1 if total - largest >= count - 1 else 0
    given, rest = [largest] + [least] * (count - 1), total - largest - least * (count - 1)
    while rest > 0:
        candidates = [i for i in range(1, count) if given[i] < largest] or [i for i in range(1, count) if given[i] < reach]
        pool, left = sum([loads[i] for i in candidates]), rest
        for i in candidates:
            addition = min(reach - given[i], max(1, left * loads[i] // pool), rest)
            given[i] = given[i] + addition
            rest = rest - addition
    return np.array(given)


def bell_draw(own_key, extent, spread, reach, shards=(), held_as=jnp.bfloat16):
    values = spread * jax.random.normal(own_key, extent, jnp.float32)
    if shards:
        values = values * steps_of(own_key, extent, shards, -0.22, 0.18)
    return jnp.clip(values, -reach, reach).astype(held_as)


def setup_inputs(seed: int = 0) -> dict:
    streams_of = jax.random.split(jax.random.key(seed), 16)
    entering = bell_draw(streams_of[0], (DOCS, NEW, D), 1.0, 6.0, ((0, 32), (1, 8)))
    moe_gain = jnp.clip(1.0 + 0.18 * jax.random.normal(streams_of[1], (D,), jnp.float32), 0.1, 1.9)
    expert_ids_keys = jax.random.split(jax.random.fold_in(streams_of[2], 1), DOCS * NEW // NEW_DEV)
    expert_ids_turns = jax.random.permutation(jax.random.fold_in(streams_of[2], 3), DOCS * NEW // NEW_DEV)
    expert_ids = jax.vmap(lambda own, number: deal_out(jax.random.fold_in(streams_of[2], 2), own, number, NEW_DEV, EXPERTS, TOP, CAP, 2))(expert_ids_keys, expert_ids_turns).reshape((DOCS, NEW, TOP))
    gate_weights = jnp.clip(jnp.exp(math.log(0.5) - 2.3025851 * jax.random.uniform(streams_of[3], (DOCS, NEW, TOP), jnp.float32) ** steps_of(streams_of[3], (DOCS, NEW, TOP), ((0, 32),), -0.2, 0.2)), 0.05, 0.5)
    w_gate = bell_draw(streams_of[4], (EXPERTS, D, FF), D ** -0.5, 0.0625, ((0, 32), (2, 8)))
    w_up = bell_draw(streams_of[5], (EXPERTS, D, FF), D ** -0.5, 0.0625, ((0, 32), (2, 8)))
    w_down = bell_draw(streams_of[6], (EXPERTS, FF, D), FF ** -0.5, 0.125, ((0, 32), (1, 8)))
    w_latent = bell_draw(streams_of[7], (D, LAT), D ** -0.5, 0.0625, ((0, 8),))
    w_rope = bell_draw(streams_of[8], (ROPE, D), D ** -0.5, 0.0625, ((1, 8),))
    latent_gain = jnp.clip(1.0 + 0.18 * jax.random.normal(streams_of[9], (LAT,), jnp.float32), 0.1, 1.9)
    prefix_len = draw_prefix_len(jax.random.fold_in(streams_of[15], 71), 0)
    cache_latent = bell_draw(streams_of[11], (DOCS, CACHE, LAT), 1.0, 4.0, ((0, 32), (1, 8)))
    cache_rope = draw_cache_rope(jax.random.fold_in(streams_of[15], 71), 0)
    query_latent = bell_draw(streams_of[13], (DOCS, NEW, H * LAT), 1.2, 7.0, ((0, 32), (1, 8)))
    query_rope = draw_query_rope(jax.random.fold_in(streams_of[15], 71), 0)
    return dict(entering=entering, moe_gain=moe_gain, expert_ids=expert_ids, gate_weights=gate_weights, w_gate=w_gate, w_up=w_up, w_down=w_down, w_latent=w_latent, w_rope=w_rope, latent_gain=latent_gain, prefix_len=prefix_len, cache_latent=cache_latent, cache_rope=cache_rope, query_latent=query_latent, query_rope=query_rope)


softmax_scale = 192 ** (-0.5)
rope_base = 10000.0

def rms_rows(values, gain):
    mean_sq = lax.optimization_barrier(jnp.mean(values * values, axis=-1, keepdims=True))
    return values * lax.rsqrt(mean_sq + 1e-06) * gain

def rotate_pairs(values, positions):
    half = values.shape[-1] // 2
    steps = jnp.arange(half, dtype=jnp.float32) * 2.0 / values.shape[-1]
    freqs = rope_base ** (-steps)
    angle = positions.astype(jnp.float32)[:, None] * freqs[None, :]
    first = values[:, :half]
    second = values[:, half:]
    cosine = jnp.cos(angle)
    sine = jnp.sin(angle)
    return jnp.concatenate([first * cosine - second * sine, second * cosine + first * sine], axis=-1)

def score_block(query_lat, query_rot, key_lat, key_rot_cols):
    lat_part = jnp.dot(query_lat, key_lat.T, preferred_element_type=jnp.float32)
    rot_part = jnp.dot(query_rot, key_rot_cols, preferred_element_type=jnp.float32)
    return (lat_part + rot_part) * softmax_scale

def reference(entering, moe_gain, expert_ids, gate_weights, w_gate, w_up, w_down, w_latent, w_rope, latent_gain, prefix_len, cache_latent, cache_rope, query_latent, query_rope):
    count_tokens = DOCS * NEW
    flat_entering = entering.reshape(count_tokens, D)
    normed = rms_rows(flat_entering.astype(jnp.float32), moe_gain).astype(jnp.bfloat16)
    routes = expert_ids.reshape(count_tokens, TOP)
    gates = gate_weights.reshape(count_tokens, TOP)
    bucket = DOCS * N_SEQ * CAP
    order = jnp.arange(count_tokens, dtype=jnp.int32)

    def one_expert(running, expert):
        hits = routes == expert
        member = jnp.any(hits, axis=1)
        weight = lax.optimization_barrier(jnp.sum(jnp.where(hits, gates, 0.0), axis=1))
        rank = jnp.cumsum(member.astype(jnp.int32)) - 1
        where_to = jnp.where(member, rank, bucket).astype(jnp.int32)
        picked = jnp.zeros((bucket,), jnp.int32).at[where_to].set(order, mode='drop')
        rows = normed[picked]
        gate = jnp.dot(rows, w_gate[expert], preferred_element_type=jnp.float32)
        upper = jnp.dot(rows, w_up[expert], preferred_element_type=jnp.float32)
        hidden = (jax.nn.silu(gate) * upper).astype(jnp.bfloat16)
        down = w_down[expert]
        summed = jnp.zeros((bucket, D), jnp.float32)
        for slice_index in range(N_SEQ):
            lower = slice_index * FF_DEV
            piece = jnp.dot(hidden[:, lower:lower + FF_DEV], down[lower:lower + FF_DEV], preferred_element_type=jnp.float32).astype(jnp.bfloat16)
            piece = lax.optimization_barrier(piece)
            summed = summed + piece.astype(jnp.float32)
        back = summed[jnp.clip(rank, 0, bucket - 1)]
        return (running + weight[:, None] * back, None)
    moe_total, _ = lax.scan(one_expert, jnp.zeros((count_tokens, D), jnp.float32), jnp.arange(EXPERTS, dtype=jnp.int32))
    layer_flat = (flat_entering.astype(jnp.float32) + moe_total).astype(jnp.bfloat16)
    latent_raw = jnp.dot(layer_flat, w_latent, preferred_element_type=jnp.float32)
    rope_raw = jnp.dot(layer_flat, w_rope.T, preferred_element_type=jnp.float32)
    new_latent = rms_rows(latent_raw, latent_gain).astype(jnp.bfloat16).reshape(DOCS, NEW, LAT)
    positions = (prefix_len[:, None] + jnp.arange(NEW, dtype=jnp.int32)[None, :]).astype(jnp.int32)
    new_rope = rotate_pairs(rope_raw, positions.reshape(-1)).astype(jnp.bfloat16).reshape(DOCS, NEW, ROPE)

    def one_doc(items):
        q_lat, q_rot, c_lat, c_rot, n_lat, n_rot, prefix = items
        query_lat = q_lat.reshape(NEW * H, LAT)
        query_rot = q_rot.reshape(NEW * H, ROPE)
        older = score_block(query_lat, query_rot, c_lat, c_rot)
        fresh = score_block(query_lat, query_rot, n_lat, n_rot.T)
        query_place = jnp.arange(NEW * H, dtype=jnp.int32) // H
        cache_ok = (jnp.arange(CACHE, dtype=jnp.int32) < prefix)[None, :]
        fresh_ok = jnp.arange(NEW, dtype=jnp.int32)[None, :] <= query_place[:, None]
        older = jnp.where(cache_ok, older, -jnp.inf)
        fresh = jnp.where(fresh_ok, fresh, -jnp.inf)
        highest = jnp.maximum(lax.optimization_barrier(jnp.max(older, axis=1)), lax.optimization_barrier(jnp.max(fresh, axis=1)))
        older_weights = jnp.exp(older - highest[:, None])
        fresh_weights = jnp.exp(fresh - highest[:, None])
        total = lax.optimization_barrier(jnp.sum(older_weights, axis=1)) + lax.optimization_barrier(jnp.sum(fresh_weights, axis=1))
        gathered = jnp.dot(older_weights.astype(jnp.bfloat16), c_lat, preferred_element_type=jnp.float32)
        gathered = gathered + jnp.dot(fresh_weights.astype(jnp.bfloat16), n_lat, preferred_element_type=jnp.float32)
        return (gathered / total[:, None]).astype(jnp.bfloat16).reshape(NEW, H * LAT)
    attention = lax.map(one_doc, (query_latent, query_rope, cache_latent, cache_rope, new_latent, new_rope, prefix_len))
    return (layer_flat.reshape(DOCS, NEW, D), attention)
```

```python
import jax
import jax.numpy as jnp
from jax import lax
from jax.sharding import PartitionSpec as P

softmax_scale = 192 ** (-0.5)
rope_base = 10000.0


def rms_rows(values, gain):
    mean_sq = jnp.mean(values * values, axis=-1, keepdims=True)
    return values * lax.rsqrt(mean_sq + 1e-06) * gain


def rotate_pairs(values, positions):
    half = values.shape[-1] // 2
    steps = jnp.arange(half, dtype=jnp.float32) * 2.0 / values.shape[-1]
    freqs = rope_base ** (-steps)
    angle = positions.astype(jnp.float32)[:, None] * freqs[None, :]
    first = values[:, :half]
    second = values[:, half:]
    cosine = jnp.cos(angle)
    sine = jnp.sin(angle)
    return jnp.concatenate(
        [first * cosine - second * sine, second * cosine + first * sine], axis=-1
    )


def score_block(query_lat, query_rot, key_lat, key_rot_cols):
    lat_part = jnp.dot(query_lat, key_lat.T, preferred_element_type=jnp.float32)
    rot_part = jnp.dot(query_rot, key_rot_cols, preferred_element_type=jnp.float32)
    return (lat_part + rot_part) * softmax_scale


def block_slots(routes, experts, capacity):
    same = (routes[:, :, None, None] == routes[None, None, :, :]).any(axis=3)
    order = jnp.arange(routes.shape[0], dtype=jnp.int32)
    earlier = order[None, :] < order[:, None]
    slots = jnp.sum((same & earlier[:, None, :]).astype(jnp.int32), axis=2)
    return routes * capacity + slots


def expert_terms(rows, gate_matrix, up_matrix, down_matrix):
    gate = jnp.dot(rows, gate_matrix, preferred_element_type=jnp.float32)
    upper = jnp.dot(rows, up_matrix, preferred_element_type=jnp.float32)
    hidden = (jax.nn.silu(gate) * upper).astype(jnp.bfloat16)
    return jnp.dot(hidden, down_matrix, preferred_element_type=jnp.float32)


def local(
    entering,
    moe_gain,
    expert_ids,
    gate_weights,
    w_gate,
    w_up,
    w_down,
    w_latent,
    w_rope,
    latent_gain,
    prefix_len,
    cache_latent,
    cache_rope,
    query_latent,
    query_rope,
):
    seq_count = lax.axis_size("seq")
    seq_place = lax.axis_index("seq")
    experts = lax.axis_size("ep")
    own_entering = entering[0]
    new_dev, width = own_entering.shape
    new = new_dev * seq_count
    capacity = 2
    prefix = prefix_len[0]
    heads = query_latent.shape[2] // cache_latent.shape[2]
    lat_width = cache_latent.shape[2]
    rot_width = cache_rope.shape[1]

    routes = lax.dynamic_slice_in_dim(expert_ids[0], seq_place * new_dev, new_dev, 0)
    gates = lax.dynamic_slice_in_dim(gate_weights[0], seq_place * new_dev, new_dev, 0)
    normed = rms_rows(own_entering.astype(jnp.float32), moe_gain).astype(jnp.bfloat16)
    targets = block_slots(routes, experts, capacity)
    total_slots = experts * capacity
    hits = targets[:, :, None] == jnp.arange(total_slots, dtype=jnp.int32)[None, None, :]
    placement = jnp.any(hits, axis=1).astype(jnp.bfloat16)
    gate_rows = jnp.sum(jnp.where(hits, gates[:, :, None], 0.0), axis=1)
    outgoing = jnp.dot(placement.T, normed, preferred_element_type=jnp.float32)
    outgoing = outgoing.astype(jnp.bfloat16).reshape(experts, capacity, width)
    arrived = lax.all_to_all(outgoing, "ep", split_axis=0, concat_axis=0, tiled=True)
    rows = lax.all_gather(arrived.reshape(total_slots, width), "seq", axis=0, tiled=True)

    older_lat = lax.all_gather(cache_latent[0], "seq", axis=0, tiled=True)
    older_rot = lax.all_gather(cache_rope[0], "seq", axis=1, tiled=True)
    query_lat = query_latent[0].reshape(new_dev * heads, lat_width)
    query_rot = query_rope[0].reshape(new_dev * heads, rot_width)
    older = score_block(query_lat, query_rot, older_lat, older_rot)
    cache_ok = (jnp.arange(older_lat.shape[0], dtype=jnp.int32) < prefix)[None, :]
    older = jnp.where(cache_ok, older, -jnp.inf)
    older_high = jnp.max(older, axis=1)
    older_weights = jnp.exp(older - older_high[:, None])
    older_total = jnp.sum(older_weights, axis=1)
    older_sum = jnp.dot(
        older_weights.astype(jnp.bfloat16), older_lat, preferred_element_type=jnp.float32
    )

    terms = expert_terms(rows, w_gate[0], w_up[0], w_down[0]).astype(jnp.bfloat16)
    summed = lax.psum_scatter(terms, "seq", scatter_dimension=0, tiled=True)
    summed = summed.reshape(experts, capacity, width)
    returned = lax.all_to_all(summed, "ep", split_axis=0, concat_axis=0, tiled=True)
    weighted = jnp.dot(
        gate_rows,
        returned.reshape(total_slots, width).astype(jnp.float32),
        precision=lax.Precision.HIGHEST,
    )
    layer_own = (own_entering.astype(jnp.float32) + weighted).astype(jnp.bfloat16)
    layer = lax.all_to_all(layer_own, "seq", split_axis=1, concat_axis=0, tiled=True)
    latent_part = jnp.dot(layer, w_latent, preferred_element_type=jnp.float32)
    rope_part = lax.dot_general(
        layer, w_rope, (((1,), (1,)), ((), ())), preferred_element_type=jnp.float32
    )
    raw = lax.psum(jnp.concatenate([latent_part, rope_part], axis=1), "seq")
    fresh_lat = rms_rows(raw[:, :lat_width], latent_gain).astype(jnp.bfloat16)
    positions = prefix + jnp.arange(new, dtype=jnp.int32)
    fresh_rot = rotate_pairs(raw[:, lat_width:], positions).astype(jnp.bfloat16)

    fresh = score_block(query_lat, query_rot, fresh_lat, fresh_rot.T)
    query_place = seq_place * new_dev + jnp.arange(new_dev * heads, dtype=jnp.int32) // heads
    fresh_ok = jnp.arange(new, dtype=jnp.int32)[None, :] <= query_place[:, None]
    fresh = jnp.where(fresh_ok, fresh, -jnp.inf)
    highest = jnp.maximum(older_high, jnp.max(fresh, axis=1))
    scale = jnp.exp(older_high - highest)
    fresh_weights = jnp.exp(fresh - highest[:, None])
    total = older_total * scale + jnp.sum(fresh_weights, axis=1)
    gathered = older_sum * scale[:, None] + jnp.dot(
        fresh_weights.astype(jnp.bfloat16), fresh_lat, preferred_element_type=jnp.float32
    )
    output = (gathered / total[:, None]).astype(jnp.bfloat16).reshape(new_dev, heads * lat_width)
    return (layer[None], output[None])


def solution(mesh):
    placed = (
        P("ep", "seq", None),
        P(),
        P("ep", None, None),
        P("ep", None, None),
        P("ep", None, "seq"),
        P("ep", None, "seq"),
        P("ep", "seq", None),
        P("seq", None),
        P(None, "seq"),
        P(),
        P("ep"),
        P("ep", "seq", None),
        P("ep", None, "seq"),
        P("ep", "seq", None),
        P("ep", "seq", None),
    )
    return jax.shard_map(
        local,
        mesh=mesh,
        in_specs=placed,
        out_specs=(P("ep", None, "seq"), P("ep", "seq", None)),
        check_vma=False,
    )
```

```python
import jax
import jax.numpy as jnp
from jax import lax
from jax.experimental import pallas as pl
from jax.experimental.pallas import tpu as pltpu
from jax.sharding import PartitionSpec as P

softmax_scale = 192 ** (-0.5)
rope_base = 10000.0
MESH = pl.DeviceIdType.MESH
SEQ = 8
YS = 4
XS = 4
ZS = 8
EPS = XS * ZS
CAP = 2
ROWS = SEQ * CAP
CHUNKS = 4
CROWS = ROWS * EPS // CHUNKS
HALF = CROWS // 2
SLICE = 896
UNITS = 256
NEW = 32
LATPAD = 640


def rms_rows(values, gain):
    mean_sq = jnp.mean(values * values, axis=-1, keepdims=True)
    return values * lax.rsqrt(mean_sq + 1e-06) * gain


def rotate_pairs(values, positions):
    half = values.shape[-1] // 2
    steps = jnp.arange(half, dtype=jnp.float32) * 2.0 / values.shape[-1]
    freqs = rope_base ** (-steps)
    angle = positions.astype(jnp.float32)[:, None] * freqs[None, :]
    first = values[:, :half]
    second = values[:, half:]
    cosine = jnp.cos(angle)
    sine = jnp.sin(angle)
    return jnp.concatenate(
        [first * cosine - second * sine, second * cosine + first * sine], axis=-1
    )


def score_block(query_lat, query_rot, key_lat, key_rot_cols):
    lat_part = jnp.dot(query_lat, key_lat.T, preferred_element_type=jnp.float32)
    rot_part = jnp.dot(query_rot, key_rot_cols, preferred_element_type=jnp.float32)
    return (lat_part + rot_part) * softmax_scale


def slot_targets(routes, doc):
    new, top = routes.shape
    blocks = new // 4
    grouped = routes.reshape(blocks, 4, top)
    same = (grouped[:, :, :, None, None] == grouped[:, None, None, :, :]).any(axis=4)
    order = jnp.arange(4, dtype=jnp.int32)
    earlier = (order[None, :] < order[:, None])[None, :, None, :]
    ranks = jnp.sum((same & earlier).astype(jnp.int32), axis=3).reshape(new, top)
    far = (routes // ZS - doc // ZS + XS) % XS * ZS + (routes % ZS - doc % ZS + ZS) % ZS
    return far * ROWS + jnp.arange(new, dtype=jnp.int32)[:, None] // 4 * CAP + ranks


def moe_kernel(
    entering,
    gain,
    tgt_cols,
    tgt,
    gates,
    w_gate,
    w_up,
    w_down,
    w_latent,
    w_rope,
    layer_out,
    raw_out,
    snd,
    rcv,
    outb,
    rows_in,
    w_in,
    w_out,
    w_lat,
    w_rot,
    part,
    sib,
    half,
    whole,
    final,
    back,
    lat_snd,
    lat_rcv,
    w_sem,
    ent_s,
    ent_r,
    go_s,
    go_r,
    y_s,
    y_r,
    rs_s,
    rs_r,
    ret_s,
    ret_r,
    lat_s,
    lat_r,
):
    s = lax.axis_index("seq")
    e = lax.axis_index("ep")
    y = s // 2
    c = s % 2
    x = e // ZS
    z = e % ZS
    other = y * 2 + 1 - c

    def at_y(dy):
        return lax.rem(y + dy + YS, YS) * 2 + c

    def pair_y(dy):
        return lax.rem(y + dy + YS, YS) * 2 + 1 - c

    def ep_plus(off):
        return lax.rem(x + off // ZS, XS) * ZS + lax.rem(z + off % ZS, ZS)

    def ep_minus(off):
        return lax.rem(x - off // ZS + XS, XS) * ZS + lax.rem(z - off % ZS + ZS, ZS)

    barrier = pltpu.get_barrier_semaphore()
    for off in range(1, EPS):
        pl.semaphore_signal(
            barrier, inc=1, device_id={"seq": s, "ep": ep_plus(off)}, device_id_type=MESH
        )
    for j in range(1, SEQ):
        pl.semaphore_signal(
            barrier, inc=1, device_id={"seq": lax.rem(s + j, SEQ), "ep": e}, device_id_type=MESH
        )

    loads = []

    def load(source, target):
        copy = pltpu.make_async_copy(source, target, w_sem.at[len(loads)])
        copy.start()
        loads.append(copy)

    for j in range(SEQ):
        load(w_gate.at[pl.ds(j * SLICE, SLICE), :], w_in.at[j, :, pl.ds(0, UNITS)])
        load(w_up.at[pl.ds(j * SLICE, SLICE), :], w_in.at[j, :, pl.ds(UNITS, UNITS)])
        load(w_down.at[:, pl.ds(j * SLICE, SLICE)], w_out.at[j])
    load(w_latent, w_lat)
    load(w_rope, w_rot)

    values = entering[...].astype(jnp.float32)
    mean_sq = jnp.mean(values * values, axis=-1, keepdims=True)
    normed = values * lax.rsqrt(mean_sq + 1e-06) * gain[...]
    normed = normed.astype(jnp.bfloat16).astype(jnp.float32)
    for j in range(SEQ):
        snd[j, 0:4, :] = values[:, j * SLICE : (j + 1) * SLICE]
        snd[j, 4:8, :] = normed[:, j * SLICE : (j + 1) * SLICE]
    pl.semaphore_wait(barrier, EPS - 1 + SEQ - 1)

    sends = []

    def remote(source, target, send_sem, recv_sem, seq, ep):
        return pltpu.make_async_remote_copy(
            src_ref=source,
            dst_ref=target,
            send_sem=send_sem,
            recv_sem=recv_sem,
            device_id={"seq": seq, "ep": ep},
            device_id_type=MESH,
        )

    def send(*args):
        copy = remote(*args)
        copy.start()
        sends.append(copy)

    def arrive(target, send_sem, recv_sem):
        remote(target, target, send_sem, recv_sem, other, e).wait_recv()

    for j in range(1, SEQ):
        to = lax.rem(s + j, SEQ)
        send(snd.at[to], rcv.at[s], ent_s.at[j], ent_r.at[j], to, e)
    rcv[s] = snd[s]
    for j in range(1, SEQ):
        arrive(rcv.at[lax.rem(s - j + SEQ, SEQ)], ent_s.at[j], ent_r.at[j])

    tokens = rcv[...].reshape(SEQ * 8, SLICE).astype(jnp.bfloat16)
    for k in range(CHUNKS):
        slots = lax.broadcasted_iota(jnp.int32, (CROWS, SEQ * 8), 0) + k * CROWS
        hit = slots == tgt_cols[0:1, :]
        for r in range(1, 8):
            hit = hit | (slots == tgt_cols[r : r + 1, :])
        place = jnp.where(hit, 1.0, 0.0).astype(jnp.bfloat16)
        outb[k * CROWS : (k + 1) * CROWS, :] = jnp.dot(
            place, tokens, preferred_element_type=jnp.float32
        ).astype(jnp.bfloat16)
        for off in range(k * EPS // CHUNKS, (k + 1) * EPS // CHUNKS):
            here = pl.ds(off * ROWS, ROWS)
            if off == 0:
                rows_in[s, here, :] = outb[here, :]
            else:
                send(
                    outb.at[here],
                    rows_in.at[s, here],
                    go_s.at[off],
                    go_r.at[off],
                    s,
                    ep_plus(off),
                )

    def rows(k):
        return pl.ds(k * CROWS, CROWS)

    def low(k):
        return pl.ds(k * CROWS, HALF)

    def high(k):
        return pl.ds(k * CROWS + HALF, HALF)

    def y_send(k, i, slice_at, which, to):
        ref = rows_in.at[slice_at, which]
        send(ref, ref, y_s.at[k, i], y_r.at[k, i], to, e)

    def y_arrive(k, i, slice_at, which):
        arrive(rows_in.at[slice_at, which], y_s.at[k, i], y_r.at[k, i])

    def gather_own(k):
        for off in range(k * EPS // CHUNKS, (k + 1) * EPS // CHUNKS):
            if off:
                arrive(rows_in.at[s, pl.ds(off * ROWS, ROWS)], go_s.at[off], go_r.at[off])
        y_send(k, 0, s, rows(k), at_y(1))
        y_send(k, 1, s, rows(k), at_y(-1))
        y_send(k, 2, s, rows(k), other)

    def gather_next(k):
        y_arrive(k, 0, at_y(-1), rows(k))
        y_send(k, 3, at_y(-1), low(k), at_y(1))
        y_send(k, 4, at_y(-1), rows(k), other)
        y_arrive(k, 1, at_y(1), rows(k))
        y_send(k, 5, at_y(1), high(k), at_y(-1))
        y_send(k, 6, at_y(1), rows(k), other)

    def gather_far(k):
        y_arrive(k, 3, at_y(2), low(k))
        y_arrive(k, 5, at_y(2), high(k))
        y_send(k, 7, at_y(2), rows(k), other)

    def compute(k):
        y_arrive(k, 2, other, rows(k))
        y_arrive(k, 4, pair_y(-1), rows(k))
        y_arrive(k, 6, pair_y(1), rows(k))
        y_arrive(k, 7, pair_y(2), rows(k))
        if k == 0:
            for copy in loads:
                copy.wait()

        def add(j, total):
            return total + jnp.dot(
                rows_in[j, rows(k), :], w_in[j], preferred_element_type=jnp.float32
            )

        total = lax.fori_loop(0, SEQ, add, jnp.zeros((CROWS, 2 * UNITS), jnp.float32))
        gate = total[:, :UNITS]
        hidden = (gate / (1.0 + jnp.exp(-gate)) * total[:, UNITS:]).astype(jnp.bfloat16)

        def down(j, carry):
            part[k, j] = jnp.dot(
                hidden, w_out[j], preferred_element_type=jnp.float32
            ).astype(jnp.bfloat16)
            return carry

        lax.fori_loop(0, SEQ, down, 0)
        for dy in (2, 1, 3, 0):
            send(
                part.at[k, pair_y(dy)], sib.at[k, dy], rs_s.at[k, dy], rs_r.at[k, dy], other, e
            )

    def plus(a, b):
        return (a.astype(jnp.float32) + b.astype(jnp.float32)).astype(jnp.bfloat16)

    def scatter_far(k):
        for dy in (2, 1, 3, 0):
            arrive(sib.at[k, dy], rs_s.at[k, dy], rs_r.at[k, dy])
            part[k, at_y(dy)] = plus(part[k, at_y(dy)], sib[k, dy])
            if dy == 2:
                far = part.at[k, at_y(2)]
                send(
                    far.at[pl.ds(0, HALF)],
                    half.at[k, 0],
                    rs_s.at[k, 4],
                    rs_r.at[k, 4],
                    at_y(1),
                    e,
                )
                send(
                    far.at[pl.ds(HALF, HALF)],
                    half.at[k, 1],
                    rs_s.at[k, 5],
                    rs_r.at[k, 5],
                    at_y(-1),
                    e,
                )

    def scatter_next(k):
        arrive(half.at[k, 0], rs_s.at[k, 4], rs_r.at[k, 4])
        part[k, at_y(1), 0:HALF, :] = plus(part[k, at_y(1), 0:HALF, :], half[k, 0])
        send(part.at[k, at_y(1)], whole.at[k, 0], rs_s.at[k, 6], rs_r.at[k, 6], at_y(1), e)
        arrive(half.at[k, 1], rs_s.at[k, 5], rs_r.at[k, 5])
        part[k, at_y(-1), HALF:CROWS, :] = plus(part[k, at_y(-1), HALF:CROWS, :], half[k, 1])
        send(part.at[k, at_y(-1)], whole.at[k, 1], rs_s.at[k, 7], rs_r.at[k, 7], at_y(-1), e)

    def give_back(k):
        arrive(whole.at[k, 0], rs_s.at[k, 6], rs_r.at[k, 6])
        arrive(whole.at[k, 1], rs_s.at[k, 7], rs_r.at[k, 7])
        final[k] = (
            part[k, s].astype(jnp.float32)
            + whole[k, 0].astype(jnp.float32)
            + whole[k, 1].astype(jnp.float32)
        ).astype(jnp.bfloat16)
        first = k * EPS // CHUNKS
        for off in range(first, (k + 1) * EPS // CHUNKS):
            here = pl.ds((off - first) * ROWS, ROWS)
            there = pl.ds(off * ROWS, ROWS)
            if off == 0:
                back[there, :] = final[k, here, :]
            else:
                send(
                    final.at[k, here],
                    back.at[there],
                    ret_s.at[off],
                    ret_r.at[off],
                    s,
                    ep_minus(off),
                )

    stages = (gather_own, gather_next, gather_far, compute, scatter_far, scatter_next, give_back)
    for step in range(CHUNKS + len(stages) - 1):
        for i in reversed(range(len(stages))):
            if 0 <= step - i < CHUNKS:
                stages[i](step - i)

    token = lax.broadcasted_iota(jnp.int32, (NEW, SEQ * 8), 0)
    column = lax.broadcasted_iota(jnp.int32, (NEW, SEQ * 8), 1)
    own = jnp.where(column == token // 4 * 8 + token % 4, 1.0, 0.0).astype(jnp.bfloat16)
    layer = jnp.dot(own, tokens, preferred_element_type=jnp.float32)
    for k in range(CHUNKS):
        slots = lax.broadcasted_iota(jnp.int32, (NEW, CROWS), 1) + k * CROWS
        share = jnp.zeros((NEW, CROWS), jnp.float32)
        for r in range(8):
            share = share + jnp.where(slots == tgt[:, r : r + 1], gates[:, r : r + 1], 0.0)
        share_high = share.astype(jnp.bfloat16)
        share_low = (share - share_high.astype(jnp.float32)).astype(jnp.bfloat16)
        for off in range(k * EPS // CHUNKS, (k + 1) * EPS // CHUNKS):
            if off:
                arrive(back.at[pl.ds(off * ROWS, ROWS)], ret_s.at[off], ret_r.at[off])
        values = back[k * CROWS : (k + 1) * CROWS, :]
        layer = layer + jnp.dot(share_high, values, preferred_element_type=jnp.float32)
        layer = layer + jnp.dot(share_low, values, preferred_element_type=jnp.float32)
    layer = layer.astype(jnp.bfloat16)
    layer_out[...] = layer
    lat_snd[:, 0:512] = jnp.dot(
        layer, w_lat[...], preferred_element_type=jnp.float32
    ).astype(jnp.bfloat16)
    rot = lax.dot_general(
        layer, w_rot[...], (((1,), (1,)), ((), ())), preferred_element_type=jnp.float32
    ).astype(jnp.bfloat16)
    lat_snd[:, 512:LATPAD] = jnp.concatenate([rot, jnp.zeros_like(rot)], axis=1)
    for j in range(1, SEQ):
        to = lax.rem(s + j, SEQ)
        send(lat_snd, lat_rcv.at[s], lat_s.at[j], lat_r.at[j], to, e)
    raw = lat_snd[...].astype(jnp.float32)
    for j in range(1, SEQ):
        place = lax.rem(s - j + SEQ, SEQ)
        arrive(lat_rcv.at[place], lat_s.at[j], lat_r.at[j])
        raw = raw + lat_rcv[place].astype(jnp.float32)
    raw_out[...] = raw
    for copy in sends:
        copy.wait_send()


def routed_layer(entering, gain, tgt_cols, tgt, gates, w_gate, w_up, w_down, w_latent, w_rope):
    bf = jnp.bfloat16
    dma = pltpu.SemaphoreType.DMA
    vmem = pl.BlockSpec(memory_space=pltpu.VMEM)
    hbm = pl.BlockSpec(memory_space=pl.ANY)
    return pl.pallas_call(
        moe_kernel,
        out_shape=(
            jax.ShapeDtypeStruct((NEW, SLICE), bf),
            jax.ShapeDtypeStruct((NEW, LATPAD), jnp.float32),
        ),
        in_specs=[vmem] * 5 + [hbm] * 5,
        out_specs=(vmem, vmem),
        scratch_shapes=[
            pltpu.VMEM((SEQ, 8, SLICE), jnp.float32),
            pltpu.VMEM((SEQ, 8, SLICE), jnp.float32),
            pltpu.VMEM((EPS * ROWS, SLICE), bf),
            pltpu.VMEM((SEQ, EPS * ROWS, SLICE), bf),
            pltpu.VMEM((SEQ, SLICE, 2 * UNITS), bf),
            pltpu.VMEM((SEQ, UNITS, SLICE), bf),
            pltpu.VMEM((SLICE, 512), bf),
            pltpu.VMEM((64, SLICE), bf),
            pltpu.VMEM((CHUNKS, SEQ, CROWS, SLICE), bf),
            pltpu.VMEM((CHUNKS, YS, CROWS, SLICE), bf),
            pltpu.VMEM((CHUNKS, 2, HALF, SLICE), bf),
            pltpu.VMEM((CHUNKS, 2, CROWS, SLICE), bf),
            pltpu.VMEM((CHUNKS, CROWS, SLICE), bf),
            pltpu.VMEM((EPS * ROWS, SLICE), bf),
            pltpu.VMEM((NEW, LATPAD), bf),
            pltpu.VMEM((SEQ, NEW, LATPAD), bf),
            dma((3 * SEQ + 2,)),
            dma((SEQ,)),
            dma((SEQ,)),
            dma((EPS,)),
            dma((EPS,)),
            dma((CHUNKS, 8)),
            dma((CHUNKS, 8)),
            dma((CHUNKS, 8)),
            dma((CHUNKS, 8)),
            dma((EPS,)),
            dma((EPS,)),
            dma((SEQ,)),
            dma((SEQ,)),
        ],
        compiler_params=pltpu.CompilerParams(
            collective_id=0, has_side_effects=True, vmem_limit_bytes=56 * 2**20
        ),
        cost_estimate=pl.CostEstimate(
            flops=6_000_000_000, bytes_accessed=14_000_000, transcendentals=131072
        ),
    )(entering, gain, tgt_cols, tgt, gates, w_gate, w_up, w_down, w_latent, w_rope)


def local(
    entering,
    moe_gain,
    expert_ids,
    gate_weights,
    w_gate,
    w_up,
    w_down,
    w_latent,
    w_rope,
    latent_gain,
    prefix_len,
    cache_latent,
    cache_rope,
    query_latent,
    query_rope,
):
    seq_count = lax.axis_size("seq")
    seq_place = lax.axis_index("seq")
    own_entering = entering[0]
    new_dev, width = own_entering.shape
    new = new_dev * seq_count
    prefix = prefix_len[0]
    heads = query_latent.shape[2] // cache_latent.shape[2]
    lat_width = cache_latent.shape[2]
    rot_width = cache_rope.shape[1]

    routes = expert_ids[0]
    tgt = slot_targets(routes, lax.axis_index("ep"))
    spaced = jnp.concatenate(
        [jnp.full((SEQ, 4, 8), -1, jnp.int32), tgt.reshape(SEQ, 4, 8)], axis=1
    )
    layer, raw = routed_layer(
        own_entering,
        moe_gain.reshape(1, width),
        spaced.reshape(SEQ * 8, 8).T,
        tgt,
        gate_weights[0],
        w_gate[0],
        w_up[0],
        w_down[0],
        w_latent,
        w_rope,
    )

    older_lat = lax.all_gather(cache_latent[0], "seq", axis=0, tiled=True)
    older_rot = lax.all_gather(cache_rope[0], "seq", axis=1, tiled=True)
    query_lat = query_latent[0].reshape(new_dev * heads, lat_width)
    query_rot = query_rope[0].reshape(new_dev * heads, rot_width)
    older = score_block(query_lat, query_rot, older_lat, older_rot)
    cache_ok = (jnp.arange(older_lat.shape[0], dtype=jnp.int32) < prefix)[None, :]
    older = jnp.where(cache_ok, older, -jnp.inf)
    older_high = jnp.max(older, axis=1)
    older_weights = jnp.exp(older - older_high[:, None])
    older_total = jnp.sum(older_weights, axis=1)
    older_sum = jnp.dot(
        older_weights.astype(jnp.bfloat16), older_lat, preferred_element_type=jnp.float32
    )

    fresh_lat = rms_rows(raw[:, :lat_width], latent_gain).astype(jnp.bfloat16)
    positions = prefix + jnp.arange(new, dtype=jnp.int32)
    fresh_rot = rotate_pairs(raw[:, lat_width : lat_width + rot_width], positions).astype(jnp.bfloat16)

    fresh = score_block(query_lat, query_rot, fresh_lat, fresh_rot.T)
    query_place = seq_place * new_dev + jnp.arange(new_dev * heads, dtype=jnp.int32) // heads
    fresh_ok = jnp.arange(new, dtype=jnp.int32)[None, :] <= query_place[:, None]
    fresh = jnp.where(fresh_ok, fresh, -jnp.inf)
    highest = jnp.maximum(older_high, jnp.max(fresh, axis=1))
    scale = jnp.exp(older_high - highest)
    fresh_weights = jnp.exp(fresh - highest[:, None])
    total = older_total * scale + jnp.sum(fresh_weights, axis=1)
    gathered = older_sum * scale[:, None] + jnp.dot(
        fresh_weights.astype(jnp.bfloat16), fresh_lat, preferred_element_type=jnp.float32
    )
    output = (gathered / total[:, None]).astype(jnp.bfloat16).reshape(new_dev, heads * lat_width)
    return (layer[None], output[None])


def solution(mesh):
    placed = (
        P("ep", "seq", None),
        P(),
        P("ep", None, None),
        P("ep", None, None),
        P("ep", None, "seq"),
        P("ep", None, "seq"),
        P("ep", "seq", None),
        P("seq", None),
        P(None, "seq"),
        P(),
        P("ep"),
        P("ep", "seq", None),
        P("ep", None, "seq"),
        P("ep", "seq", None),
        P("ep", "seq", None),
    )
    return jax.shard_map(
        local,
        mesh=mesh,
        in_specs=placed,
        out_specs=(P("ep", None, "seq"), P("ep", "seq", None)),
        check_vma=False,
    )
```

```python
import math

import jax
import jax.numpy as jnp
from jax import lax
from jax.experimental import pallas as pl
from jax.experimental.pallas import tpu as pltpu
from jax.sharding import PartitionSpec as P

softmax_scale = 192 ** (-0.5)
rope_base = 10000.0
MESH = pl.DeviceIdType.MESH
SEQ = 8
YS = 4
XS = 4
ZS = 8
EPS = XS * ZS
CAP = 2
ROWS = SEQ * CAP
PAIRS = ((0, 1), (6, 3), (5, 4), (7, 2))
SPOT = {dz: 2 * k + p for k, pair in enumerate(PAIRS) for p, dz in enumerate(pair)}
CHUNKS = len(PAIRS)
CROWS = ROWS * EPS // CHUNKS
XROWS = CROWS // XS
SLICE = 896
UNITS = 256
NEW = 32
LATPAD = 640
TOP = 8
HEADS = 128
LAT = 512
ROPE = 64
CACHE = 1024
KEYS = CACHE // SEQ


def moe_kernel(
    entering,
    gain,
    ids,
    gates,
    w_gate,
    w_up,
    w_down,
    w_latent,
    w_rope,
    latent_gain,
    prefix,
    cache_lat,
    cache_rot,
    query_lat,
    query_rot,
    layer_out,
    att_out,
    idbuf,
    info,
    info_in,
    snd,
    rcv,
    zs,
    zin,
    share_hi,
    share_lo,
    xs,
    rows_in,
    w_in,
    w_out,
    w_lat,
    w_rot,
    part,
    sib,
    whole,
    final,
    xback,
    zsum,
    zback,
    far_snd,
    far_rcv,
    lat_snd,
    lat_rcv,
    key_lat,
    key_rot,
    old_high,
    old_total,
    old_sum,
    w_sem,
    info_s,
    info_r,
    ent_s,
    ent_r,
    z_s,
    z_r,
    x_s,
    x_r,
    y_s,
    y_r,
    rs_s,
    rs_r,
    xb_s,
    xb_r,
    zb_s,
    zb_r,
    lat_s,
    lat_r,
    key_s,
    key_r,
):
    s = lax.axis_index("seq")
    e = lax.axis_index("ep")
    y = s // 2
    c = s % 2
    x = e // ZS
    z = e % ZS
    other = y * 2 + 1 - c

    def at_y(dy):
        return lax.rem(y + dy + YS, YS) * 2 + c

    def pair_y(dy):
        return lax.rem(y + dy + YS, YS) * 2 + 1 - c

    def at_z(dz):
        return x * ZS + lax.rem(z + dz + ZS, ZS)

    def at_x(dx):
        return lax.rem(x + dx + XS, XS) * ZS + z

    barrier = pltpu.get_barrier_semaphore()

    def greet(seq, ep):
        pl.semaphore_signal(
            barrier, inc=1, device_id={"seq": seq, "ep": ep}, device_id_type=MESH
        )

    for j in range(1, SEQ):
        greet(lax.rem(s + j, SEQ), e)
    for j in range(1, ZS):
        greet(s, at_z(j))
    for j in range(1, XS):
        greet(s, at_x(j))

    loads = []

    def load(source, target):
        copy = pltpu.make_async_copy(source, target, w_sem.at[len(loads)])
        copy.start()
        loads.append(copy)

    for j in range(SEQ):
        load(w_gate.at[pl.ds(j * SLICE, SLICE), :], w_in.at[j, :, pl.ds(0, UNITS)])
        load(w_up.at[pl.ds(j * SLICE, SLICE), :], w_in.at[j, :, pl.ds(UNITS, UNITS)])
        load(w_down.at[:, pl.ds(j * SLICE, SLICE)], w_out.at[j])
    load(w_latent, w_lat)
    load(w_rope, w_rot)

    values = entering[...].astype(jnp.float32)
    mean_sq = jnp.mean(values * values, axis=-1, keepdims=True)
    normed = values * lax.rsqrt(mean_sq + 1e-06) * gain[...]
    for j in range(SEQ):
        far = (j + SEQ // 2) % SEQ
        mine = normed[:, j * SLICE : (j + 1) * SLICE]
        snd[j] = jnp.concatenate(
            [
                values[:, j * SLICE : (j + 1) * SLICE],
                mine,
                normed[:, far * SLICE : (far + 1) * SLICE],
                jnp.zeros_like(mine),
            ],
            axis=0,
        ).astype(jnp.bfloat16)

    idbuf[...] = jnp.full((TOP, 128), -1, jnp.int32)
    idbuf[:, 0:NEW] = ids[...]
    routes = idbuf[...]
    lane = lax.broadcasted_iota(jnp.int32, (TOP, 128), 1)
    rank = jnp.zeros((TOP, 128), jnp.int32)
    for i in range(1, 4):
        earlier = pltpu.roll(routes, i, 1)
        for r in range(TOP):
            same = (routes == earlier[r : r + 1, :]) & (lane % 4 >= i)
            rank = rank + same.astype(jnp.int32)
    code = ((routes % ZS - z + ZS) % ZS) * (XS * ROWS) + ((routes // ZS - x + XS) % XS) * ROWS
    code = code + lane // 4 * CAP + rank
    info[0:TOP, :] = code.astype(jnp.float32)
    info[TOP : 2 * TOP, :] = jnp.zeros((TOP, 128), jnp.float32)
    info[TOP : 2 * TOP, 0:NEW] = gates[...]
    pl.semaphore_wait(barrier, SEQ - 1 + ZS - 1 + XS - 1)

    sends = []

    def remote(source, target, send_sem, recv_sem, seq, ep):
        return pltpu.make_async_remote_copy(
            src_ref=source,
            dst_ref=target,
            send_sem=send_sem,
            recv_sem=recv_sem,
            device_id={"seq": seq, "ep": ep},
            device_id_type=MESH,
        )

    def send(*args):
        copy = remote(*args)
        copy.start()
        sends.append(copy)

    def arrive(target, send_sem, recv_sem):
        remote(target, target, send_sem, recv_sem, other, e).wait_recv()

    for j in range(1, SEQ):
        to = lax.rem(s + j, SEQ)
        send(snd.at[to], rcv.at[s], ent_s.at[j], ent_r.at[j], to, e)
    rcv[s] = snd[s]
    info_in[0] = info[...]
    for k in range(CHUNKS):
        for p in range(2):
            spot = 2 * k + p
            if spot:
                send(
                    info,
                    info_in.at[spot],
                    info_s.at[spot],
                    info_r.at[spot],
                    s,
                    at_z(PAIRS[k][p]),
                )

    def key_refs(place):
        return (
            key_lat.at[pl.ds(place * KEYS, KEYS)],
            key_rot.at[:, pl.ds(place * KEYS, KEYS)],
        )

    key_lat[pl.ds(s * KEYS, KEYS), :] = cache_lat[...]
    key_rot[:, pl.ds(s * KEYS, KEYS)] = cache_rot[...]

    def key_send(n, place, to):
        for i, ref in enumerate(key_refs(place)):
            send(ref, ref, key_s.at[n, i], key_r.at[n, i], to, e)

    def key_arrive(n, place):
        for i, ref in enumerate(key_refs(place)):
            arrive(ref, key_s.at[n, i], key_r.at[n, i])

    for j in range(1, SEQ):
        arrive(rcv.at[lax.rem(s - j + SEQ, SEQ)], ent_s.at[j], ent_r.at[j])

    tokens = rcv[...].reshape(SEQ * 16, SLICE)

    def pick(first):
        token = lax.broadcasted_iota(jnp.int32, (NEW, SEQ * 16), 0)
        column = lax.broadcasted_iota(jnp.int32, (NEW, SEQ * 16), 1)
        chosen = column == token // 4 * 16 + token % 4 + first
        return jnp.dot(
            jnp.where(chosen, 1.0, 0.0).astype(jnp.bfloat16),
            tokens,
            preferred_element_type=jnp.float32,
        )

    for i in range(2):
        zs[i] = pick(4 + 4 * i).astype(jnp.bfloat16)

    def z_send(i, dz, ref, way):
        spot = SPOT[dz]
        send(ref, zin.at[i, spot], z_s.at[i, spot], z_r.at[i, spot], s, at_z(way))

    def z_pass(i, dz, way):
        z_send(i, (dz + way) % ZS, zin.at[i, SPOT[dz]], way)

    for i in range(2):
        z_send(i, 1, zs.at[i], 1)
        z_send(i, ZS - 1, zs.at[i], -1)
        zin[i, 0] = zs[i]
    for n, to in enumerate((at_y(1), at_y(-1), at_y(2), other)):
        key_send(n, s, to)

    def relay(hop):
        for i in range(2):
            for dz, way in ((hop, 1), (ZS - hop, -1)):
                if hop < ZS // 2:
                    arrive(zin.at[i, SPOT[dz]], z_s.at[i, SPOT[dz]], z_r.at[i, SPOT[dz]])
                    if hop < ZS // 2 - 1 or (i == 0) == (way == 1):
                        z_pass(i, dz, way)
            if hop == ZS // 2:
                arrive(zin.at[i, SPOT[hop]], z_s.at[i, SPOT[hop]], z_r.at[i, SPOT[hop]])

    def keys_on(unused):
        for n, dy in ((0, -1), (1, 1), (2, 2)):
            key_arrive(n, at_y(dy))
            key_send(4 + n, at_y(dy), other)

    slices = (s, at_y(2))

    def rows(k):
        return pl.ds(k * CROWS, CROWS)

    def routed(k):
        codes, shares = [], []
        for p in range(2):
            spot = 2 * k + p
            if spot:
                arrive(info_in.at[spot], info_s.at[spot], info_r.at[spot])
            local = info_in[spot, 0:TOP, 0:NEW] - float(PAIRS[k][p] * XS * ROWS)
            inside = (local >= 0.0) & (local < float(XS * ROWS))
            row = local + jnp.floor(local * (1.0 / ROWS)) * ROWS + float(p * ROWS)
            codes.append(jnp.where(inside, row, -1.0))
            shares.append(info_in[spot, TOP : 2 * TOP, 0:NEW])
        code = jnp.concatenate(codes, axis=1)
        share = jnp.concatenate(shares, axis=1)
        at = lax.broadcasted_iota(jnp.int32, (CROWS, 2 * NEW), 0).astype(jnp.float32)
        place = jnp.zeros((CROWS, 2 * NEW), jnp.float32)
        weigh = jnp.zeros((CROWS, 2 * NEW), jnp.float32)
        for r in range(TOP):
            hit = at == code[r : r + 1, :]
            place = place + jnp.where(hit, 1.0, 0.0)
            weigh = weigh + jnp.where(hit, share[r : r + 1, :], 0.0)
        place = place.astype(jnp.bfloat16)
        high = weigh.astype(jnp.bfloat16)
        share_hi[k] = high
        share_lo[k] = (weigh - high.astype(jnp.float32)).astype(jnp.bfloat16)
        for i in range(2):
            both = zin[i, 2 * k : 2 * k + 2].reshape(2 * NEW, SLICE)
            xs[i, k] = jnp.dot(place, both, preferred_element_type=jnp.float32).astype(
                jnp.bfloat16
            )
            for dx in (1, 3, 2):
                send(
                    xs.at[i, k, pl.ds(dx * XROWS, XROWS)],
                    rows_in.at[slices[i], pl.ds(k * CROWS + dx * XROWS, XROWS)],
                    x_s.at[k, i, dx],
                    x_r.at[k, i, dx],
                    s,
                    at_x(dx),
                )
            rows_in[slices[i], pl.ds(k * CROWS, XROWS), :] = xs[i, k, 0:XROWS, :]

    def y_send(k, i, slice_at, to):
        ref = rows_in.at[slice_at, rows(k)]
        send(ref, ref, y_s.at[k, i], y_r.at[k, i], to, e)

    def y_arrive(k, i, slice_at):
        arrive(rows_in.at[slice_at, rows(k)], y_s.at[k, i], y_r.at[k, i])

    def gather_own(k):
        for i in range(2):
            for dx in (1, 3, 2):
                arrive(
                    rows_in.at[slices[i], pl.ds(k * CROWS + dx * XROWS, XROWS)],
                    x_s.at[k, i, dx],
                    x_r.at[k, i, dx],
                )
            if i == 0:
                y_send(k, 0, s, at_y(1))
                y_send(k, 1, s, at_y(-1))
                y_send(k, 2, s, other)
            else:
                y_send(k, 3, slices[1], other)

    def gather_next(k):
        y_arrive(k, 0, at_y(-1))
        y_send(k, 4, at_y(-1), other)
        y_arrive(k, 1, at_y(1))
        y_send(k, 5, at_y(1), other)

    def compute(k):
        y_arrive(k, 2, other)
        y_arrive(k, 3, pair_y(2))
        y_arrive(k, 4, pair_y(-1))
        y_arrive(k, 5, pair_y(1))
        if k == 0:
            for copy in loads:
                copy.wait()

        def add(j, total):
            return total + jnp.dot(
                rows_in[j, rows(k), :], w_in[j], preferred_element_type=jnp.float32
            )

        total = lax.fori_loop(0, SEQ, add, jnp.zeros((CROWS, 2 * UNITS), jnp.float32))
        gate = total[:, :UNITS]
        hidden = (gate / (1.0 + jnp.exp(-gate)) * total[:, UNITS:]).astype(jnp.bfloat16)

        def down(j, carry):
            part[k, j] = jnp.dot(
                hidden, w_out[j], preferred_element_type=jnp.float32
            ).astype(jnp.bfloat16)
            return carry

        lax.fori_loop(0, SEQ, down, 0)
        for dy in (1, 3, 2, 0):
            send(
                part.at[k, pair_y(dy)], sib.at[k, dy], rs_s.at[k, dy], rs_r.at[k, dy], other, e
            )

    def plus(a, b):
        return (a.astype(jnp.float32) + b.astype(jnp.float32)).astype(jnp.bfloat16)

    def x_return(k, i):
        for dx in (1, 3, 2):
            send(
                final.at[k, i, pl.ds(dx * XROWS, XROWS)],
                xback.at[i, k, pl.ds(dx * XROWS, XROWS)],
                xb_s.at[k, i, dx],
                xb_r.at[k, i, dx],
                s,
                at_x(-dx),
            )
        xback[i, k, 0:XROWS, :] = final[k, i, 0:XROWS, :]

    def scatter_pair(k):
        for i, dy in ((0, 1), (1, 3)):
            arrive(sib.at[k, dy], rs_s.at[k, dy], rs_r.at[k, dy])
            part[k, at_y(dy)] = plus(part[k, at_y(dy)], sib[k, dy])
            send(
                part.at[k, at_y(dy)],
                whole.at[k, i],
                rs_s.at[k, 4 + i],
                rs_r.at[k, 4 + i],
                at_y(dy),
                e,
            )
        arrive(sib.at[k, 2], rs_s.at[k, 2], rs_r.at[k, 2])
        final[k, 1] = plus(part[k, at_y(2)], sib[k, 2])
        x_return(k, 1)
        arrive(sib.at[k, 0], rs_s.at[k, 0], rs_r.at[k, 0])

    def give_back(k):
        arrive(whole.at[k, 0], rs_s.at[k, 4], rs_r.at[k, 4])
        arrive(whole.at[k, 1], rs_s.at[k, 5], rs_r.at[k, 5])
        final[k, 0] = (
            part[k, s].astype(jnp.float32)
            + sib[k, 0].astype(jnp.float32)
            + whole[k, 0].astype(jnp.float32)
            + whole[k, 1].astype(jnp.float32)
        ).astype(jnp.bfloat16)
        x_return(k, 0)

    def weigh_back(k):
        for i in (1, 0):
            for dx in (1, 3, 2):
                arrive(
                    xback.at[i, k, pl.ds(dx * XROWS, XROWS)],
                    xb_s.at[k, i, dx],
                    xb_r.at[k, i, dx],
                )
            got = xback[i, k]
            over = (((0,), (0,)), ((), ()))
            summed = lax.dot_general(
                share_hi[k], got, over, preferred_element_type=jnp.float32
            ) + lax.dot_general(share_lo[k], got, over, preferred_element_type=jnp.float32)
            zsum[i, 2 * k : 2 * k + 2] = summed.astype(jnp.bfloat16).reshape(2, NEW, SLICE)
            for p in range(2):
                spot = 2 * k + p
                if spot:
                    send(
                        zsum.at[i, spot],
                        zback.at[i, spot],
                        zb_s.at[i, spot],
                        zb_r.at[i, spot],
                        s,
                        at_z(-PAIRS[k][p]),
                    )
                else:
                    zback[i, 0] = zsum[i, 0]

    def scores(b, keys, rot_keys, turned):
        here = slice(b * HEADS, (b + 1) * HEADS)
        over = (((1,), (1,)), ((), ()))
        lat_part = lax.dot_general(
            query_lat[here, :], keys, over, preferred_element_type=jnp.float32
        )
        if turned:
            rot_part = lax.dot_general(
                query_rot[here, :], rot_keys, over, preferred_element_type=jnp.float32
            )
        else:
            rot_part = jnp.dot(query_rot[here, :], rot_keys, preferred_element_type=jnp.float32)
        return (lat_part + rot_part) * softmax_scale

    def cached(b):
        if b == 0:
            for n, dy in ((3, 0), (4, -1), (5, 1), (6, 2)):
                key_arrive(n, pair_y(dy))
        here = slice(b * HEADS, (b + 1) * HEADS)
        older = scores(b, key_lat[...], key_rot[...], False)
        place = lax.broadcasted_iota(jnp.int32, (HEADS, CACHE), 1)
        older = jnp.where(place < prefix[0, 0], older, -jnp.inf)
        high = jnp.max(older, axis=1, keepdims=True)
        weights = jnp.exp(older - high)
        old_high[here, :] = high
        old_total[here, :] = jnp.sum(weights, axis=1, keepdims=True)
        old_sum[here, :] = jnp.dot(
            weights.astype(jnp.bfloat16), key_lat[...], preferred_element_type=jnp.float32
        )

    own, nxt, comp, pair, give, weigh = (
        gather_own,
        gather_next,
        compute,
        scatter_pair,
        give_back,
        weigh_back,
    )
    schedule = (
        ((relay, 1), (routed, 0), (relay, 2), (relay, 3), (routed, 1), (own, 0), (relay, 4))
        + ((routed, 2), (nxt, 0), (own, 1), (routed, 3), (keys_on, 0))
        + ((comp, 0), (nxt, 1), (own, 2), (cached, 0), (pair, 0), (comp, 1), (nxt, 2), (own, 3))
        + ((cached, 1), (give, 0), (pair, 1), (comp, 2), (nxt, 3), (cached, 2))
        + ((weigh, 0), (give, 1), (pair, 2), (comp, 3), (cached, 3))
        + ((weigh, 1), (give, 2), (pair, 3), (weigh, 2), (give, 3), (weigh, 3))
    )
    for stage, k in schedule:
        stage(k)

    def collect(i):
        total = zback[i, 0].astype(jnp.float32)
        for spot in range(1, ZS):
            arrive(zback.at[i, spot], zb_s.at[i, spot], zb_r.at[i, spot])
            total = total + zback[i, spot].astype(jnp.float32)
        return total

    index = lax.broadcasted_iota(jnp.int32, (NEW, ROPE // 2), 1).astype(jnp.float32)
    position = lax.broadcasted_iota(jnp.int32, (NEW, ROPE // 2), 0) + prefix[0, 0]
    angle = position.astype(jnp.float32) * jnp.exp(index * (-2.0 / ROPE * math.log(rope_base)))
    cosine = jnp.cos(angle)
    sine = jnp.sin(angle)
    far_snd[...] = collect(1).astype(jnp.bfloat16)
    send(far_snd, far_rcv, lat_s.at[0], lat_r.at[0], slices[1], e)
    layer = pick(0) + collect(0)
    arrive(far_rcv, lat_s.at[0], lat_r.at[0])
    layer = (layer + far_rcv[...].astype(jnp.float32)).astype(jnp.bfloat16)
    layer_out[...] = layer
    lat_snd[:, 0:LAT] = jnp.dot(
        layer, w_lat[...], preferred_element_type=jnp.float32
    ).astype(jnp.bfloat16)
    rot = lax.dot_general(
        layer, w_rot[...], (((1,), (1,)), ((), ())), preferred_element_type=jnp.float32
    ).astype(jnp.bfloat16)
    lat_snd[:, LAT:LATPAD] = jnp.concatenate([rot, jnp.zeros_like(rot)], axis=1)
    for j in range(1, SEQ):
        to = lax.rem(s + j, SEQ)
        send(lat_snd, lat_rcv.at[s], lat_s.at[j], lat_r.at[j], to, e)
    raw = lat_snd[...].astype(jnp.float32)
    for j in range(1, SEQ):
        place = lax.rem(s - j + SEQ, SEQ)
        arrive(lat_rcv.at[place], lat_s.at[j], lat_r.at[j])
        raw = raw + lat_rcv[place].astype(jnp.float32)
    fresh = raw[:, 0:LAT]
    fresh_sq = jnp.mean(fresh * fresh, axis=-1, keepdims=True)
    fresh = (fresh * lax.rsqrt(fresh_sq + 1e-06) * latent_gain[...]).astype(jnp.bfloat16)
    first = raw[:, LAT : LAT + ROPE // 2]
    second = raw[:, LAT + ROPE // 2 : LAT + ROPE]
    rotated = jnp.concatenate(
        [first * cosine - second * sine, second * cosine + first * sine], axis=1
    ).astype(jnp.bfloat16)
    for b in range(4):
        here = slice(b * HEADS, (b + 1) * HEADS)
        newer = scores(b, fresh, rotated, True)
        place = lax.broadcasted_iota(jnp.int32, (HEADS, NEW), 1)
        newer = jnp.where(place <= s * 4 + b, newer, -jnp.inf)
        high = jnp.maximum(old_high[here, :], jnp.max(newer, axis=1, keepdims=True))
        scale = jnp.exp(old_high[here, :] - high)
        weights = jnp.exp(newer - high)
        total = old_total[here, :] * scale + jnp.sum(weights, axis=1, keepdims=True)
        summed = old_sum[here, :] * scale + jnp.dot(
            weights.astype(jnp.bfloat16), fresh, preferred_element_type=jnp.float32
        )
        att_out[here, :] = (summed / total).astype(jnp.bfloat16)
    for copy in sends:
        copy.wait_send()


def block(*arrays):
    bf = jnp.bfloat16
    f32 = jnp.float32
    dma = pltpu.SemaphoreType.DMA
    vmem = pl.BlockSpec(memory_space=pltpu.VMEM)
    hbm = pl.BlockSpec(memory_space=pl.ANY)
    return pl.pallas_call(
        moe_kernel,
        out_shape=(
            jax.ShapeDtypeStruct((NEW, SLICE), bf),
            jax.ShapeDtypeStruct((4 * HEADS, LAT), bf),
        ),
        in_specs=[vmem] * 4
        + [hbm] * 5
        + [vmem, pl.BlockSpec(memory_space=pltpu.SMEM)]
        + [vmem] * 4,
        out_specs=(vmem, vmem),
        scratch_shapes=[
            pltpu.VMEM((TOP, 128), jnp.int32),
            pltpu.VMEM((2 * TOP, 128), f32),
            pltpu.VMEM((ZS, 2 * TOP, 128), f32),
            pltpu.VMEM((SEQ, 16, SLICE), bf),
            pltpu.VMEM((SEQ, 16, SLICE), bf),
            pltpu.VMEM((2, NEW, SLICE), bf),
            pltpu.VMEM((2, ZS, NEW, SLICE), bf),
            pltpu.VMEM((CHUNKS, CROWS, 2 * NEW), bf),
            pltpu.VMEM((CHUNKS, CROWS, 2 * NEW), bf),
            pltpu.VMEM((2, CHUNKS, CROWS, SLICE), bf),
            pltpu.VMEM((SEQ, EPS * ROWS, SLICE), bf),
            pltpu.VMEM((SEQ, SLICE, 2 * UNITS), bf),
            pltpu.VMEM((SEQ, UNITS, SLICE), bf),
            pltpu.VMEM((SLICE, 512), bf),
            pltpu.VMEM((64, SLICE), bf),
            pltpu.VMEM((CHUNKS, SEQ, CROWS, SLICE), bf),
            pltpu.VMEM((CHUNKS, YS, CROWS, SLICE), bf),
            pltpu.VMEM((CHUNKS, 2, CROWS, SLICE), bf),
            pltpu.VMEM((CHUNKS, 2, CROWS, SLICE), bf),
            pltpu.VMEM((2, CHUNKS, CROWS, SLICE), bf),
            pltpu.VMEM((2, ZS, NEW, SLICE), bf),
            pltpu.VMEM((2, ZS, NEW, SLICE), bf),
            pltpu.VMEM((NEW, SLICE), bf),
            pltpu.VMEM((NEW, SLICE), bf),
            pltpu.VMEM((NEW, LATPAD), bf),
            pltpu.VMEM((SEQ, NEW, LATPAD), bf),
            pltpu.VMEM((CACHE, LAT), bf),
            pltpu.VMEM((ROPE, CACHE), bf),
            pltpu.VMEM((4 * HEADS, 1), f32),
            pltpu.VMEM((4 * HEADS, 1), f32),
            pltpu.VMEM((4 * HEADS, LAT), f32),
            dma((3 * SEQ + 2,)),
            dma((ZS,)),
            dma((ZS,)),
            dma((SEQ,)),
            dma((SEQ,)),
            dma((2, ZS)),
            dma((2, ZS)),
            dma((CHUNKS, 2, XS)),
            dma((CHUNKS, 2, XS)),
            dma((CHUNKS, 6)),
            dma((CHUNKS, 6)),
            dma((CHUNKS, 6)),
            dma((CHUNKS, 6)),
            dma((CHUNKS, 2, XS)),
            dma((CHUNKS, 2, XS)),
            dma((2, ZS)),
            dma((2, ZS)),
            dma((SEQ,)),
            dma((SEQ,)),
            dma((7, 2)),
            dma((7, 2)),
        ],
        compiler_params=pltpu.CompilerParams(
            collective_id=0, has_side_effects=True, vmem_limit_bytes=56 * 2**20
        ),
        cost_estimate=pl.CostEstimate(
            flops=6_000_000_000, bytes_accessed=14_000_000, transcendentals=131072
        ),
    )(*arrays)


def local(
    entering,
    moe_gain,
    expert_ids,
    gate_weights,
    w_gate,
    w_up,
    w_down,
    w_latent,
    w_rope,
    latent_gain,
    prefix_len,
    cache_latent,
    cache_rope,
    query_latent,
    query_rope,
):
    layer, output = block(
        entering[0],
        moe_gain.reshape(1, -1),
        expert_ids[0].T,
        gate_weights[0].T,
        w_gate[0],
        w_up[0],
        w_down[0],
        w_latent,
        w_rope,
        latent_gain.reshape(1, LAT),
        prefix_len.reshape(1, 1),
        cache_latent[0],
        cache_rope[0],
        query_latent.reshape(4 * HEADS, LAT),
        query_rope.reshape(4 * HEADS, ROPE),
    )
    return (layer[None], output.reshape(1, 4, HEADS * LAT))


def solution(mesh):
    placed = (
        P("ep", "seq", None),
        P(),
        P("ep", None, None),
        P("ep", None, None),
        P("ep", None, "seq"),
        P("ep", None, "seq"),
        P("ep", "seq", None),
        P("seq", None),
        P(None, "seq"),
        P(),
        P("ep"),
        P("ep", "seq", None),
        P("ep", None, "seq"),
        P("ep", "seq", None),
        P("ep", "seq", None),
    )
    return jax.shard_map(
        local,
        mesh=mesh,
        in_specs=placed,
        out_specs=(P("ep", None, "seq"), P("ep", "seq", None)),
        check_vma=False,
    )
```

```python
import math

import jax
import jax.numpy as jnp
from jax import lax
from jax.experimental import pallas as pl
from jax.experimental.pallas import tpu as pltpu
from jax.sharding import PartitionSpec as P

softmax_scale = 192 ** (-0.5)
rope_base = 10000.0
MESH = pl.DeviceIdType.MESH
SEQ = 8
YS = 4
XS = 4
ZS = 8
EPS = XS * ZS
CAP = 2
ROWS = SEQ * CAP
PAIRS = ((0, 1), (6, 3), (5, 4), (7, 2))
GROUP = len(PAIRS[0])
SPOT = {dz: GROUP * k + p for k, pair in enumerate(PAIRS) for p, dz in enumerate(pair)}
CHUNKS = len(PAIRS)
CROWS = ROWS * EPS // CHUNKS
XROWS = CROWS // XS
SLICE = 896
UNITS = 256
NEW = 32
LATPAD = 640
TOP = 8
HEADS = 128
LAT = 512
ROPE = 64
CACHE = 1024
KEYS = CACHE // SEQ


def moe_kernel(
    entering,
    gain,
    ids,
    gates,
    w_gate,
    w_up,
    w_down,
    w_latent,
    w_rope,
    latent_gain,
    prefix,
    cache_lat,
    cache_rot,
    query_lat,
    query_rot,
    layer_out,
    att_out,
    idbuf,
    info,
    info_in,
    snd,
    rcv,
    zs,
    zin,
    places,
    share_hi,
    share_lo,
    xs,
    rows_in,
    w_in,
    w_out,
    w_lat,
    w_rot,
    part,
    sib,
    whole,
    final,
    xback,
    zsum,
    zback,
    far_snd,
    far_rcv,
    lat_snd,
    lat_rcv,
    key_lat,
    key_rot,
    turned_lat,
    turned_rot,
    zero_rot,
    old_high,
    old_total,
    old_sum,
    w_sem,
    info_s,
    info_r,
    ent_s,
    ent_r,
    z_s,
    z_r,
    x_s,
    x_r,
    y_s,
    y_r,
    rs_s,
    rs_r,
    xb_s,
    xb_r,
    zb_s,
    zb_r,
    lat_s,
    lat_r,
    key_s,
    key_r,
):
    s = lax.axis_index("seq")
    e = lax.axis_index("ep")
    y = s // 2
    c = s % 2
    x = e // ZS
    z = e % ZS
    other = y * 2 + 1 - c

    def at_y(dy):
        return lax.rem(y + dy + YS, YS) * 2 + c

    def pair_y(dy):
        return lax.rem(y + dy + YS, YS) * 2 + 1 - c

    def at_z(dz):
        return x * ZS + lax.rem(z + dz + ZS, ZS)

    def at_x(dx):
        return lax.rem(x + dx + XS, XS) * ZS + z

    barrier = pltpu.get_barrier_semaphore()

    def greet(seq, ep):
        pl.semaphore_signal(
            barrier, inc=1, device_id={"seq": seq, "ep": ep}, device_id_type=MESH
        )

    for j in range(1, SEQ):
        greet(lax.rem(s + j, SEQ), e)
    for j in range(1, ZS):
        greet(s, at_z(j))
    for j in range(1, XS):
        greet(s, at_x(j))

    loads = []

    def load(source, target):
        copy = pltpu.make_async_copy(source, target, w_sem.at[len(loads)])
        copy.start()
        loads.append(copy)

    for j in range(SEQ):
        load(w_gate.at[pl.ds(j * SLICE, SLICE), :], w_in.at[j, :, pl.ds(0, UNITS)])
        load(w_up.at[pl.ds(j * SLICE, SLICE), :], w_in.at[j, :, pl.ds(UNITS, UNITS)])
        load(w_down.at[:, pl.ds(j * SLICE, SLICE)], w_out.at[j])
    load(w_latent, w_lat)
    load(w_rope, w_rot)

    values = entering[...].astype(jnp.float32)
    mean_sq = jnp.mean(values * values, axis=-1, keepdims=True)
    normed = values * lax.rsqrt(mean_sq + 1e-06) * gain[...]
    for j in range(SEQ):
        far = (j + SEQ // 2) % SEQ
        mine = normed[:, j * SLICE : (j + 1) * SLICE]
        snd[j] = jnp.concatenate(
            [
                values[:, j * SLICE : (j + 1) * SLICE],
                mine,
                normed[:, far * SLICE : (far + 1) * SLICE],
                jnp.zeros_like(mine),
            ],
            axis=0,
        ).astype(jnp.bfloat16)

    idbuf[...] = jnp.full((TOP, 128), -1, jnp.int32)
    idbuf[:, 0:NEW] = ids[...]
    routes = idbuf[...]
    lane = lax.broadcasted_iota(jnp.int32, (TOP, 128), 1)
    rank = jnp.zeros((TOP, 128), jnp.int32)
    for i in range(1, 4):
        earlier = pltpu.roll(routes, i, 1)
        for r in range(TOP):
            same = (routes == earlier[r : r + 1, :]) & (lane % 4 >= i)
            rank = rank + same.astype(jnp.int32)
    code = ((routes % ZS - z + ZS) % ZS) * (XS * ROWS) + ((routes // ZS - x + XS) % XS) * ROWS
    code = code + lane // 4 * CAP + rank
    info[0:TOP, :] = code.astype(jnp.float32)
    info[TOP : 2 * TOP, :] = jnp.zeros((TOP, 128), jnp.float32)
    info[TOP : 2 * TOP, 0:NEW] = gates[...]
    pl.semaphore_wait(barrier, SEQ - 1 + ZS - 1 + XS - 1)

    sends = []

    def remote(source, target, send_sem, recv_sem, seq, ep):
        return pltpu.make_async_remote_copy(
            src_ref=source,
            dst_ref=target,
            send_sem=send_sem,
            recv_sem=recv_sem,
            device_id={"seq": seq, "ep": ep},
            device_id_type=MESH,
        )

    def send(*args):
        copy = remote(*args)
        copy.start()
        sends.append(copy)

    def arrive(target, send_sem, recv_sem):
        remote(target, target, send_sem, recv_sem, other, e).wait_recv()

    for j in range(1, SEQ):
        to = lax.rem(s + j, SEQ)
        send(snd.at[to], rcv.at[s], ent_s.at[j], ent_r.at[j], to, e)
    rcv[s] = snd[s]
    info_in[0] = info[...]
    for k in range(CHUNKS):
        for p in range(GROUP):
            spot = GROUP * k + p
            if spot:
                send(
                    info,
                    info_in.at[spot],
                    info_s.at[spot],
                    info_r.at[spot],
                    s,
                    at_z(PAIRS[k][p]),
                )

    def key_refs(place):
        return (
            key_lat.at[pl.ds(place * KEYS, KEYS)],
            key_rot.at[:, pl.ds(place * KEYS, KEYS)],
        )

    key_lat[pl.ds(s * KEYS, KEYS), :] = cache_lat[...]
    key_rot[:, pl.ds(s * KEYS, KEYS)] = cache_rot[...]

    def turn(g, carry):
        for odd in range(2):
            pieces = []
            for i in range(4):
                at = ((g * 4 + i) * 2 + odd) * LAT
                piece = query_lat[0:4, pl.ds(pl.multiple_of(at, LAT), LAT)]
                pieces.append(piece.astype(jnp.float32))
            at = pl.multiple_of(odd * 2 * HEADS + g * 16, 16)
            turned_lat[pl.ds(at, 16), :] = jnp.concatenate(pieces, axis=0).astype(jnp.bfloat16)
        pieces = []
        for i in range(4):
            at = pl.multiple_of((g * 4 + i) * 2 * ROPE, 2 * ROPE)
            pieces.append(query_rot[0:4, pl.ds(at, 2 * ROPE)].astype(jnp.float32))
        at = pl.multiple_of(g * 16, 16)
        turned_rot[pl.ds(at, 16), :] = jnp.concatenate(pieces, axis=0).astype(jnp.bfloat16)
        return carry

    def queries(n):
        if n == 0:
            zero_rot[...] = jnp.zeros_like(zero_rot)
        lax.fori_loop(4 * n, 4 * n + 4, turn, 0)

    def key_send(n, place, to):
        for i, ref in enumerate(key_refs(place)):
            send(ref, ref, key_s.at[n, i], key_r.at[n, i], to, e)

    def key_arrive(n, place):
        for i, ref in enumerate(key_refs(place)):
            arrive(ref, key_s.at[n, i], key_r.at[n, i])

    for j in range(1, SEQ):
        arrive(rcv.at[lax.rem(s - j + SEQ, SEQ)], ent_s.at[j], ent_r.at[j])

    tokens = rcv[...].reshape(SEQ * 16, SLICE)

    def pick(first):
        token = lax.broadcasted_iota(jnp.int32, (NEW, SEQ * 16), 0)
        column = lax.broadcasted_iota(jnp.int32, (NEW, SEQ * 16), 1)
        chosen = column == token // 4 * 16 + token % 4 + first
        return jnp.dot(
            jnp.where(chosen, 1.0, 0.0).astype(jnp.bfloat16),
            tokens,
            preferred_element_type=jnp.float32,
        )

    for i in range(2):
        zs[i] = pick(4 + 4 * i).astype(jnp.bfloat16)

    def z_send(i, dz, ref, way):
        spot = SPOT[dz]
        send(ref, zin.at[i, spot], z_s.at[i, spot], z_r.at[i, spot], s, at_z(way))

    def z_pass(i, dz, way):
        z_send(i, (dz + way) % ZS, zin.at[i, SPOT[dz]], way)

    def z_start(i):
        z_send(i, 1, zs.at[i], 1)
        z_send(i, ZS - 1, zs.at[i], -1)

    z_start(0)
    for i in range(2):
        zin[i, 0] = zs[i]
    for n, to in enumerate((at_y(1), at_y(-1), at_y(2), other)):
        key_send(n, s, to)

    def relays(i, hop):
        for dz, way in ((hop, 1), (ZS - hop, -1)):
            if hop < ZS // 2:
                arrive(zin.at[i, SPOT[dz]], z_s.at[i, SPOT[dz]], z_r.at[i, SPOT[dz]])
                if hop < ZS // 2 - 1 or (i == 0) == (way == 1):
                    z_pass(i, dz, way)
        if hop == ZS // 2:
            arrive(zin.at[i, SPOT[hop]], z_s.at[i, SPOT[hop]], z_r.at[i, SPOT[hop]])

    def relay(hop):
        relays(0, hop)

    def far_relay(hop):
        if hop:
            relays(1, hop)
        else:
            z_start(1)

    def keys_on(unused):
        for n, dy in ((0, -1), (1, 1), (2, 2)):
            key_arrive(n, at_y(dy))
            key_send(4 + n, at_y(dy), other)

    slices = (s, at_y(2))

    def rows(k):
        return pl.ds(k * CROWS, CROWS)

    def routed(k):
        codes, shares = [], []
        for p in range(GROUP):
            spot = GROUP * k + p
            if spot:
                arrive(info_in.at[spot], info_s.at[spot], info_r.at[spot])
            local = info_in[spot, 0:TOP, 0:NEW] - float(PAIRS[k][p] * XS * ROWS)
            inside = (local >= 0.0) & (local < float(XS * ROWS))
            row = local + jnp.floor(local * (1.0 / ROWS)) * ((GROUP - 1) * ROWS) + float(p * ROWS)
            codes.append(jnp.where(inside, row, -1.0))
            shares.append(info_in[spot, TOP : 2 * TOP, 0:NEW])
        code = jnp.concatenate(codes, axis=1)
        share = jnp.concatenate(shares, axis=1)
        at = lax.broadcasted_iota(jnp.int32, (CROWS, GROUP * NEW), 0).astype(jnp.float32)
        place = jnp.zeros((CROWS, GROUP * NEW), jnp.float32)
        weigh = jnp.zeros((CROWS, GROUP * NEW), jnp.float32)
        for r in range(TOP):
            hit = at == code[r : r + 1, :]
            place = place + jnp.where(hit, 1.0, 0.0)
            weigh = weigh + jnp.where(hit, share[r : r + 1, :], 0.0)
        places[k] = place.astype(jnp.bfloat16)
        high = weigh.astype(jnp.bfloat16)
        share_hi[k] = high
        share_lo[k] = (weigh - high.astype(jnp.float32)).astype(jnp.bfloat16)
        x_go(k, 0)

    def far_routed(k):
        x_go(k, 1)

    def x_go(k, i):
        both = zin[i, GROUP * k : GROUP * (k + 1)].reshape(GROUP * NEW, SLICE)
        xs[i, k] = jnp.dot(places[k], both, preferred_element_type=jnp.float32).astype(
            jnp.bfloat16
        )
        for dx in (1, 3, 2):
            send(
                xs.at[i, k, pl.ds(dx * XROWS, XROWS)],
                rows_in.at[slices[i], pl.ds(k * CROWS + dx * XROWS, XROWS)],
                x_s.at[k, i, dx],
                x_r.at[k, i, dx],
                s,
                at_x(dx),
            )
        rows_in[slices[i], pl.ds(k * CROWS, XROWS), :] = xs[i, k, 0:XROWS, :]

    def y_send(k, i, slice_at, to):
        ref = rows_in.at[slice_at, rows(k)]
        send(ref, ref, y_s.at[k, i], y_r.at[k, i], to, e)

    def y_arrive(k, i, slice_at):
        arrive(rows_in.at[slice_at, rows(k)], y_s.at[k, i], y_r.at[k, i])

    def x_arrive(k, i):
        for dx in (1, 3, 2):
            arrive(
                rows_in.at[slices[i], pl.ds(k * CROWS + dx * XROWS, XROWS)],
                x_s.at[k, i, dx],
                x_r.at[k, i, dx],
            )

    def gather_own(k):
        x_arrive(k, 0)
        y_send(k, 0, s, at_y(1))
        y_send(k, 1, s, at_y(-1))
        y_send(k, 2, s, other)

    def gather_far(k):
        x_arrive(k, 1)
        y_send(k, 3, slices[1], other)

    def gather_next(k):
        y_arrive(k, 0, at_y(-1))
        y_send(k, 4, at_y(-1), other)
        y_arrive(k, 1, at_y(1))
        y_send(k, 5, at_y(1), other)

    def compute(k):
        y_arrive(k, 2, other)
        y_arrive(k, 3, pair_y(2))
        y_arrive(k, 4, pair_y(-1))
        y_arrive(k, 5, pair_y(1))
        if k == 0:
            for copy in loads:
                copy.wait()

        def add(j, total):
            return total + jnp.dot(
                rows_in[j, rows(k), :], w_in[j], preferred_element_type=jnp.float32
            )

        total = lax.fori_loop(0, SEQ, add, jnp.zeros((CROWS, 2 * UNITS), jnp.float32))
        gate = total[:, :UNITS]
        hidden = (gate / (1.0 + jnp.exp(-gate)) * total[:, UNITS:]).astype(jnp.bfloat16)

        def down(j, carry):
            part[k, j] = jnp.dot(
                hidden, w_out[j], preferred_element_type=jnp.float32
            ).astype(jnp.bfloat16)
            return carry

        lax.fori_loop(0, SEQ, down, 0)
        for dy in (1, 3, 2, 0):
            send(
                part.at[k, pair_y(dy)], sib.at[k, dy], rs_s.at[k, dy], rs_r.at[k, dy], other, e
            )

    def plus(a, b):
        return (a.astype(jnp.float32) + b.astype(jnp.float32)).astype(jnp.bfloat16)

    def x_return(k, i):
        for dx in (1, 3, 2):
            send(
                final.at[k, i, pl.ds(dx * XROWS, XROWS)],
                xback.at[i, k, pl.ds(dx * XROWS, XROWS)],
                xb_s.at[k, i, dx],
                xb_r.at[k, i, dx],
                s,
                at_x(-dx),
            )
        xback[i, k, 0:XROWS, :] = final[k, i, 0:XROWS, :]

    def scatter_pair(k):
        for i, dy in ((0, 1), (1, 3)):
            arrive(sib.at[k, dy], rs_s.at[k, dy], rs_r.at[k, dy])
            part[k, at_y(dy)] = plus(part[k, at_y(dy)], sib[k, dy])
            send(
                part.at[k, at_y(dy)],
                whole.at[k, i],
                rs_s.at[k, 4 + i],
                rs_r.at[k, 4 + i],
                at_y(dy),
                e,
            )
        arrive(sib.at[k, 2], rs_s.at[k, 2], rs_r.at[k, 2])
        final[k, 1] = plus(part[k, at_y(2)], sib[k, 2])
        x_return(k, 1)
        arrive(sib.at[k, 0], rs_s.at[k, 0], rs_r.at[k, 0])

    def give_back(k):
        arrive(whole.at[k, 0], rs_s.at[k, 4], rs_r.at[k, 4])
        arrive(whole.at[k, 1], rs_s.at[k, 5], rs_r.at[k, 5])
        final[k, 0] = (
            part[k, s].astype(jnp.float32)
            + sib[k, 0].astype(jnp.float32)
            + whole[k, 0].astype(jnp.float32)
            + whole[k, 1].astype(jnp.float32)
        ).astype(jnp.bfloat16)
        x_return(k, 0)

    def weigh_back(k):
        for i in (1, 0):
            for dx in (1, 3, 2):
                arrive(
                    xback.at[i, k, pl.ds(dx * XROWS, XROWS)],
                    xb_s.at[k, i, dx],
                    xb_r.at[k, i, dx],
                )
            got = xback[i, k]
            over = (((0,), (0,)), ((), ()))
            summed = lax.dot_general(
                share_hi[k], got, over, preferred_element_type=jnp.float32
            ) + lax.dot_general(share_lo[k], got, over, preferred_element_type=jnp.float32)
            zsum[i, GROUP * k : GROUP * (k + 1)] = summed.astype(jnp.bfloat16).reshape(GROUP, NEW, SLICE)
            for p in range(GROUP):
                spot = GROUP * k + p
                if spot:
                    send(
                        zsum.at[i, spot],
                        zback.at[i, spot],
                        zb_s.at[i, spot],
                        zb_r.at[i, spot],
                        s,
                        at_z(-PAIRS[k][p]),
                    )
                else:
                    zback[i, 0] = zsum[i, 0]

    def scores(b, keys, rot_keys):
        over = (((1,), (1,)), ((), ()))
        lat_part = lax.dot_general(
            turned_lat[b * HEADS : (b + 1) * HEADS, :],
            keys,
            over,
            preferred_element_type=jnp.float32,
        )
        half = b % 2
        rot_part = jnp.dot(
            turned_rot[half * HEADS : (half + 1) * HEADS, :],
            rot_keys,
            preferred_element_type=jnp.float32,
        )
        return (lat_part + rot_part) * softmax_scale

    def cached(b):
        if b == 0:
            for n, dy in ((3, 0), (4, -1), (5, 1), (6, 2)):
                key_arrive(n, pair_y(dy))
        here = slice(b * HEADS, (b + 1) * HEADS)
        if b < 2:
            rot_keys = jnp.concatenate([key_rot[...], zero_rot[...]], axis=0)
        else:
            rot_keys = jnp.concatenate([zero_rot[...], key_rot[...]], axis=0)
        older = scores(b, key_lat[...], rot_keys)
        place = lax.broadcasted_iota(jnp.int32, (HEADS, CACHE), 1)
        older = jnp.where(place < prefix[0, 0], older, -jnp.inf)
        high = jnp.max(older, axis=1, keepdims=True)
        weights = jnp.exp(older - high)
        old_high[here, :] = high
        old_total[here, :] = jnp.sum(weights, axis=1, keepdims=True)
        old_sum[here, :] = jnp.dot(
            weights.astype(jnp.bfloat16), key_lat[...], preferred_element_type=jnp.float32
        )

    own, nxt, comp, pair, give, weigh = (
        gather_own,
        gather_next,
        compute,
        scatter_pair,
        give_back,
        weigh_back,
    )
    schedule = (
        (relay, 1),
        (far_relay, 0),
        (routed, 0),
        (queries, 0),
        (relay, 2),
        (far_relay, 1),
        (own, 0),
        (relay, 3),
        (far_routed, 0),
        (routed, 1),
        (queries, 1),
        (far_relay, 2),
        (keys_on, 0),
        (relay, 4),
        (far_relay, 3),
        (gather_far, 0),
        (queries, 2),
        (nxt, 0),
        (own, 1),
        (far_routed, 1),
        (routed, 2),
        (far_relay, 4),
        (queries, 3),
        (comp, 0),
        (gather_far, 1),
        (nxt, 1),
        (own, 2),
        (far_routed, 2),
        (routed, 3),
        (pair, 0),
        (cached, 0),
        (comp, 1),
        (gather_far, 2),
        (nxt, 2),
        (own, 3),
        (far_routed, 3),
        (give, 0),
        (pair, 1),
        (cached, 1),
        (comp, 2),
        (gather_far, 3),
        (nxt, 3),
        (weigh, 0),
        (give, 1),
        (pair, 2),
        (cached, 2),
        (comp, 3),
        (weigh, 1),
        (give, 2),
        (pair, 3),
        (cached, 3),
        (weigh, 2),
        (give, 3),
        (weigh, 3),
    )
    for stage, k in schedule:
        stage(k)

    def collect(i):
        total = zback[i, 0].astype(jnp.float32)
        for spot in range(1, ZS):
            arrive(zback.at[i, spot], zb_s.at[i, spot], zb_r.at[i, spot])
            total = total + zback[i, spot].astype(jnp.float32)
        return total

    index = lax.broadcasted_iota(jnp.int32, (NEW, ROPE // 2), 1).astype(jnp.float32)
    position = lax.broadcasted_iota(jnp.int32, (NEW, ROPE // 2), 0) + prefix[0, 0]
    angle = position.astype(jnp.float32) * jnp.exp(index * (-2.0 / ROPE * math.log(rope_base)))
    cosine = jnp.cos(angle)
    sine = jnp.sin(angle)
    far_snd[...] = collect(1).astype(jnp.bfloat16)
    send(far_snd, far_rcv, lat_s.at[0], lat_r.at[0], slices[1], e)
    layer = pick(0) + collect(0)
    arrive(far_rcv, lat_s.at[0], lat_r.at[0])
    layer = (layer + far_rcv[...].astype(jnp.float32)).astype(jnp.bfloat16)
    layer_out[...] = layer
    lat_snd[:, 0:LAT] = jnp.dot(
        layer, w_lat[...], preferred_element_type=jnp.float32
    ).astype(jnp.bfloat16)
    rot = lax.dot_general(
        layer, w_rot[...], (((1,), (1,)), ((), ())), preferred_element_type=jnp.float32
    ).astype(jnp.bfloat16)
    lat_snd[:, LAT:LATPAD] = jnp.concatenate([rot, jnp.zeros_like(rot)], axis=1)
    for j in range(1, SEQ):
        to = lax.rem(s + j, SEQ)
        send(lat_snd, lat_rcv.at[s], lat_s.at[j], lat_r.at[j], to, e)
    for copy in sends[: 1 - SEQ]:
        copy.wait_send()
    raw = lat_snd[...].astype(jnp.float32)
    for j in range(1, SEQ):
        place = lax.rem(s - j + SEQ, SEQ)
        arrive(lat_rcv.at[place], lat_s.at[j], lat_r.at[j])
        raw = raw + lat_rcv[place].astype(jnp.float32)
    fresh = raw[:, 0:LAT]
    fresh_sq = jnp.mean(fresh * fresh, axis=-1, keepdims=True)
    fresh = (fresh * lax.rsqrt(fresh_sq + 1e-06) * latent_gain[...]).astype(jnp.bfloat16)
    first = raw[:, LAT : LAT + ROPE // 2]
    second = raw[:, LAT + ROPE // 2 : LAT + ROPE]
    rotated = jnp.concatenate(
        [first * cosine - second * sine, second * cosine + first * sine], axis=1
    ).T.astype(jnp.bfloat16)
    for b in range(4):
        here = slice(b * HEADS, (b + 1) * HEADS)
        blank = jnp.zeros((ROPE, NEW), jnp.bfloat16)
        both = [rotated, blank] if b < 2 else [blank, rotated]
        newer = scores(b, fresh, jnp.concatenate(both, axis=0))
        place = lax.broadcasted_iota(jnp.int32, (HEADS, NEW), 1)
        asker = lax.broadcasted_iota(jnp.int32, (HEADS, NEW), 0) % 4 + s * 4
        newer = jnp.where(place <= asker, newer, -jnp.inf)
        high = jnp.maximum(old_high[here, :], jnp.max(newer, axis=1, keepdims=True))
        scale = jnp.exp(old_high[here, :] - high)
        weights = jnp.exp(newer - high)
        total = old_total[here, :] * scale + jnp.sum(weights, axis=1, keepdims=True)
        summed = old_sum[here, :] * scale + jnp.dot(
            weights.astype(jnp.bfloat16), fresh, preferred_element_type=jnp.float32
        )
        result = summed * (1.0 / total)
        for i in range(HEADS // 4):
            head = (b % 2 * (HEADS // 4) + i) * 2 + b // 2
            att_out[:, head * LAT : (head + 1) * LAT] = result[4 * i : 4 * i + 4, :].astype(
                jnp.bfloat16
            )
    for copy in sends[1 - SEQ :]:
        copy.wait_send()


def block(*arrays):
    bf = jnp.bfloat16
    f32 = jnp.float32
    dma = pltpu.SemaphoreType.DMA
    vmem = pl.BlockSpec(memory_space=pltpu.VMEM)
    hbm = pl.BlockSpec(memory_space=pl.ANY)
    return pl.pallas_call(
        moe_kernel,
        out_shape=(
            jax.ShapeDtypeStruct((NEW, SLICE), bf),
            jax.ShapeDtypeStruct((4, HEADS * LAT), bf),
        ),
        in_specs=[vmem] * 4
        + [hbm] * 5
        + [vmem, pl.BlockSpec(memory_space=pltpu.SMEM)]
        + [vmem] * 4,
        out_specs=(vmem, vmem),
        scratch_shapes=[
            pltpu.VMEM((TOP, 128), jnp.int32),
            pltpu.VMEM((2 * TOP, 128), f32),
            pltpu.VMEM((ZS, 2 * TOP, 128), f32),
            pltpu.VMEM((SEQ, 16, SLICE), bf),
            pltpu.VMEM((SEQ, 16, SLICE), bf),
            pltpu.VMEM((2, NEW, SLICE), bf),
            pltpu.VMEM((2, ZS, NEW, SLICE), bf),
            pltpu.VMEM((CHUNKS, CROWS, GROUP * NEW), bf),
            pltpu.VMEM((CHUNKS, CROWS, GROUP * NEW), bf),
            pltpu.VMEM((CHUNKS, CROWS, GROUP * NEW), bf),
            pltpu.VMEM((2, CHUNKS, CROWS, SLICE), bf),
            pltpu.VMEM((SEQ, EPS * ROWS, SLICE), bf),
            pltpu.VMEM((SEQ, SLICE, 2 * UNITS), bf),
            pltpu.VMEM((SEQ, UNITS, SLICE), bf),
            pltpu.VMEM((SLICE, 512), bf),
            pltpu.VMEM((64, SLICE), bf),
            pltpu.VMEM((CHUNKS, SEQ, CROWS, SLICE), bf),
            pltpu.VMEM((CHUNKS, YS, CROWS, SLICE), bf),
            pltpu.VMEM((CHUNKS, 2, CROWS, SLICE), bf),
            pltpu.VMEM((CHUNKS, 2, CROWS, SLICE), bf),
            pltpu.VMEM((2, CHUNKS, CROWS, SLICE), bf),
            pltpu.VMEM((2, ZS, NEW, SLICE), bf),
            pltpu.VMEM((2, ZS, NEW, SLICE), bf),
            pltpu.VMEM((NEW, SLICE), bf),
            pltpu.VMEM((NEW, SLICE), bf),
            pltpu.VMEM((NEW, LATPAD), bf),
            pltpu.VMEM((SEQ, NEW, LATPAD), bf),
            pltpu.VMEM((CACHE, LAT), bf),
            pltpu.VMEM((ROPE, CACHE), bf),
            pltpu.VMEM((4 * HEADS, LAT), bf),
            pltpu.VMEM((2 * HEADS, 2 * ROPE), bf),
            pltpu.VMEM((ROPE, CACHE), bf),
            pltpu.VMEM((4 * HEADS, 1), f32),
            pltpu.VMEM((4 * HEADS, 1), f32),
            pltpu.VMEM((4 * HEADS, LAT), f32),
            dma((3 * SEQ + 2,)),
            dma((ZS,)),
            dma((ZS,)),
            dma((SEQ,)),
            dma((SEQ,)),
            dma((2, ZS)),
            dma((2, ZS)),
            dma((CHUNKS, 2, XS)),
            dma((CHUNKS, 2, XS)),
            dma((CHUNKS, 6)),
            dma((CHUNKS, 6)),
            dma((CHUNKS, 6)),
            dma((CHUNKS, 6)),
            dma((CHUNKS, 2, XS)),
            dma((CHUNKS, 2, XS)),
            dma((2, ZS)),
            dma((2, ZS)),
            dma((SEQ,)),
            dma((SEQ,)),
            dma((7, 2)),
            dma((7, 2)),
        ],
        compiler_params=pltpu.CompilerParams(
            collective_id=0, has_side_effects=True, vmem_limit_bytes=56 * 2**20
        ),
        cost_estimate=pl.CostEstimate(
            flops=6_000_000_000, bytes_accessed=14_000_000, transcendentals=131072
        ),
    )(*arrays)


def local(
    entering,
    moe_gain,
    expert_ids,
    gate_weights,
    w_gate,
    w_up,
    w_down,
    w_latent,
    w_rope,
    latent_gain,
    prefix_len,
    cache_latent,
    cache_rope,
    query_latent,
    query_rope,
):
    layer, output = block(
        entering[0],
        moe_gain.reshape(1, -1),
        expert_ids[0].T,
        gate_weights[0].T,
        w_gate[0],
        w_up[0],
        w_down[0],
        w_latent,
        w_rope,
        latent_gain.reshape(1, LAT),
        prefix_len.reshape(1, 1),
        cache_latent[0],
        cache_rope[0],
        query_latent[0],
        query_rope[0],
    )
    return (layer[None], output[None])


def solution(mesh):
    placed = (
        P("ep", "seq", None),
        P(),
        P("ep", None, None),
        P("ep", None, None),
        P("ep", None, "seq"),
        P("ep", None, "seq"),
        P("ep", "seq", None),
        P("seq", None),
        P(None, "seq"),
        P(),
        P("ep"),
        P("ep", "seq", None),
        P("ep", None, "seq"),
        P("ep", "seq", None),
        P("ep", "seq", None),
    )
    return jax.shard_map(
        local,
        mesh=mesh,
        in_specs=placed,
        out_specs=(P("ep", None, "seq"), P("ep", "seq", None)),
        check_vma=False,
    )
```

```python
import math

import jax
import jax.numpy as jnp
from jax import lax
from jax.experimental import pallas as pl
from jax.experimental.pallas import tpu as pltpu
from jax.sharding import PartitionSpec as P

softmax_scale = 192 ** (-0.5)
rope_base = 10000.0
MESH = pl.DeviceIdType.MESH
SEQ = 8
YS = 4
XS = 4
ZS = 8
EPS = XS * ZS
CAP = 2
ROWS = SEQ * CAP
PAIRS = ((0, 1), (7, 2), (6, 3), (5, 4))
GROUP = len(PAIRS[0])
SPOT = {dz: GROUP * k + p for k, pair in enumerate(PAIRS) for p, dz in enumerate(pair)}
CHUNKS = len(PAIRS)
CROWS = ROWS * EPS // CHUNKS
XROWS = CROWS // XS
SLICE = 896
UNITS = 256
NEW = 32
LATPAD = 640
TOP = 8
HEADS = 128
LAT = 512
ROPE = 64
CACHE = 1024
KEYS = CACHE // SEQ


def moe_kernel(
    entering,
    gain,
    ids,
    gates,
    w_gate,
    w_up,
    w_down,
    w_latent,
    w_rope,
    latent_gain,
    prefix,
    cache_lat,
    cache_rot,
    query_lat,
    query_rot,
    layer_out,
    att_out,
    idbuf,
    info,
    info_in,
    snd,
    rcv,
    zs,
    zin,
    places,
    share_hi,
    share_lo,
    xs,
    rows_in,
    w_in,
    w_out,
    w_lat,
    w_rot,
    part,
    sums,
    sib,
    whole,
    final,
    xback,
    zsum,
    zback,
    far_snd,
    far_rcv,
    lat_snd,
    lat_rcv,
    key_lat,
    key_rot,
    turned_lat,
    turned_rot,
    zero_rot,
    old_high,
    old_total,
    old_sum,
    w_sem,
    info_s,
    info_r,
    ent_s,
    ent_r,
    z_s,
    z_r,
    x_s,
    x_r,
    y_s,
    y_r,
    rs_s,
    rs_r,
    xb_s,
    xb_r,
    zb_s,
    zb_r,
    lat_s,
    lat_r,
    key_s,
    key_r,
):
    s = lax.axis_index("seq")
    e = lax.axis_index("ep")
    y = s // 2
    c = s % 2
    x = e // ZS
    z = e % ZS
    other = y * 2 + 1 - c

    def at_y(dy):
        return lax.rem(y + dy + YS, YS) * 2 + c

    def pair_y(dy):
        return lax.rem(y + dy + YS, YS) * 2 + 1 - c

    def at_z(dz):
        return x * ZS + lax.rem(z + dz + ZS, ZS)

    def at_x(dx):
        return lax.rem(x + dx + XS, XS) * ZS + z

    barrier = pltpu.get_barrier_semaphore()

    def greet(seq, ep):
        pl.semaphore_signal(
            barrier, inc=1, device_id={"seq": seq, "ep": ep}, device_id_type=MESH
        )

    for j in range(1, SEQ):
        greet(lax.rem(s + j, SEQ), e)
    for j in range(1, ZS):
        greet(s, at_z(j))
    for j in range(1, XS):
        greet(s, at_x(j))

    loads = []

    def load(source, target):
        copy = pltpu.make_async_copy(source, target, w_sem.at[len(loads)])
        copy.start()
        loads.append(copy)

    for j in range(SEQ):
        load(w_gate.at[pl.ds(j * SLICE, SLICE), :], w_in.at[j, :, pl.ds(0, UNITS)])
        load(w_up.at[pl.ds(j * SLICE, SLICE), :], w_in.at[j, :, pl.ds(UNITS, UNITS)])
        load(w_down.at[:, pl.ds(j * SLICE, SLICE)], w_out.at[j])
    load(w_latent, w_lat)
    load(w_rope, w_rot)

    values = entering[...].astype(jnp.float32)
    mean_sq = jnp.mean(values * values, axis=-1, keepdims=True)
    normed = values * lax.rsqrt(mean_sq + 1e-06) * gain[...]
    for j in range(SEQ):
        far = (j + SEQ // 2) % SEQ
        mine = normed[:, j * SLICE : (j + 1) * SLICE]
        snd[j] = jnp.concatenate(
            [
                values[:, j * SLICE : (j + 1) * SLICE],
                mine,
                normed[:, far * SLICE : (far + 1) * SLICE],
                jnp.zeros_like(mine),
            ],
            axis=0,
        ).astype(jnp.bfloat16)

    idbuf[...] = jnp.full((TOP, 128), -1, jnp.int32)
    idbuf[:, 0:NEW] = ids[...]
    routes = idbuf[...]
    lane = lax.broadcasted_iota(jnp.int32, (TOP, 128), 1)
    rank = jnp.zeros((TOP, 128), jnp.int32)
    for i in range(1, 4):
        earlier = pltpu.roll(routes, i, 1)
        for r in range(TOP):
            same = (routes == earlier[r : r + 1, :]) & (lane % 4 >= i)
            rank = rank + same.astype(jnp.int32)
    code = ((routes % ZS - z + ZS) % ZS) * (XS * ROWS) + ((routes // ZS - x + XS) % XS) * ROWS
    code = code + lane // 4 * CAP + rank
    info[0:TOP, :] = code.astype(jnp.float32)
    info[TOP : 2 * TOP, :] = jnp.zeros((TOP, 128), jnp.float32)
    info[TOP : 2 * TOP, 0:NEW] = gates[...]
    pl.semaphore_wait(barrier, SEQ - 1 + ZS - 1 + XS - 1)

    sends = []

    def remote(source, target, send_sem, recv_sem, seq, ep):
        return pltpu.make_async_remote_copy(
            src_ref=source,
            dst_ref=target,
            send_sem=send_sem,
            recv_sem=recv_sem,
            device_id={"seq": seq, "ep": ep},
            device_id_type=MESH,
        )

    def send(*args):
        copy = remote(*args)
        copy.start()
        sends.append(copy)

    def arrive(target, send_sem, recv_sem):
        remote(target, target, send_sem, recv_sem, other, e).wait_recv()

    for j in range(1, SEQ):
        to = lax.rem(s + j, SEQ)
        send(snd.at[to], rcv.at[s], ent_s.at[j], ent_r.at[j], to, e)
    rcv[s] = snd[s]
    info_in[0] = info[...]
    for k in range(CHUNKS):
        for p in range(GROUP):
            spot = GROUP * k + p
            if spot:
                send(
                    info,
                    info_in.at[spot],
                    info_s.at[spot],
                    info_r.at[spot],
                    s,
                    at_z(PAIRS[k][p]),
                )

    def key_refs(place):
        return (
            key_lat.at[pl.ds(place * KEYS, KEYS)],
            key_rot.at[:, pl.ds(place * KEYS, KEYS)],
        )

    key_lat[pl.ds(s * KEYS, KEYS), :] = cache_lat[...]
    key_rot[:, pl.ds(s * KEYS, KEYS)] = cache_rot[...]

    def turn(g, carry):
        for odd in range(2):
            pieces = []
            for i in range(4):
                at = ((g * 4 + i) * 2 + odd) * LAT
                piece = query_lat[0:4, pl.ds(pl.multiple_of(at, LAT), LAT)]
                pieces.append(piece.astype(jnp.float32))
            at = pl.multiple_of(odd * 2 * HEADS + g * 16, 16)
            turned_lat[pl.ds(at, 16), :] = jnp.concatenate(pieces, axis=0).astype(jnp.bfloat16)
        pieces = []
        for i in range(4):
            at = pl.multiple_of((g * 4 + i) * 2 * ROPE, 2 * ROPE)
            pieces.append(query_rot[0:4, pl.ds(at, 2 * ROPE)].astype(jnp.float32))
        at = pl.multiple_of(g * 16, 16)
        turned_rot[pl.ds(at, 16), :] = jnp.concatenate(pieces, axis=0).astype(jnp.bfloat16)
        return carry

    def queries(n):
        if n == 0:
            zero_rot[...] = jnp.zeros_like(zero_rot)
        lax.fori_loop(4 * n, 4 * n + 4, turn, 0)

    def key_send(n, place, to):
        for i, ref in enumerate(key_refs(place)):
            send(ref, ref, key_s.at[n, i], key_r.at[n, i], to, e)

    def key_arrive(n, place):
        for i, ref in enumerate(key_refs(place)):
            arrive(ref, key_s.at[n, i], key_r.at[n, i])

    for j in range(1, SEQ):
        arrive(rcv.at[lax.rem(s - j + SEQ, SEQ)], ent_s.at[j], ent_r.at[j])

    tokens = rcv[...].reshape(SEQ * 16, SLICE)

    def pick(first):
        token = lax.broadcasted_iota(jnp.int32, (NEW, SEQ * 16), 0)
        column = lax.broadcasted_iota(jnp.int32, (NEW, SEQ * 16), 1)
        chosen = column == token // 4 * 16 + token % 4 + first
        return jnp.dot(
            jnp.where(chosen, 1.0, 0.0).astype(jnp.bfloat16),
            tokens,
            preferred_element_type=jnp.float32,
        )

    for i in range(2):
        zs[i] = pick(4 + 4 * i).astype(jnp.bfloat16)

    def z_send(i, dz, ref, way):
        spot = SPOT[dz]
        send(ref, zin.at[i, spot], z_s.at[i, spot], z_r.at[i, spot], s, at_z(way))

    def z_pass(i, dz, way):
        z_send(i, (dz + way) % ZS, zin.at[i, SPOT[dz]], way)

    def z_start(i):
        z_send(i, 1, zs.at[i], 1)
        z_send(i, ZS - 1, zs.at[i], -1)

    z_start(0)
    for i in range(2):
        zin[i, 0] = zs[i]
    for n, to in enumerate((at_y(1), at_y(-1), at_y(2), other)):
        key_send(n, s, to)

    def relays(i, hop):
        for dz, way in ((hop, 1), (ZS - hop, -1)):
            if hop < ZS // 2:
                arrive(zin.at[i, SPOT[dz]], z_s.at[i, SPOT[dz]], z_r.at[i, SPOT[dz]])
                if hop < ZS // 2 - 1 or (i == 0) == (way == 1):
                    z_pass(i, dz, way)
        if hop == ZS // 2:
            arrive(zin.at[i, SPOT[hop]], z_s.at[i, SPOT[hop]], z_r.at[i, SPOT[hop]])

    def relay(hop):
        relays(0, hop)

    def far_relay(hop):
        if hop:
            relays(1, hop)
        else:
            z_start(1)

    def keys_on(unused):
        for n, dy in ((0, -1), (1, 1), (2, 2)):
            key_arrive(n, at_y(dy))
            key_send(4 + n, at_y(dy), other)

    slices = (s, at_y(2))

    def rows(k):
        return pl.ds(k * CROWS, CROWS)

    def routed(k):
        codes, shares = [], []
        for p in range(GROUP):
            spot = GROUP * k + p
            if spot:
                arrive(info_in.at[spot], info_s.at[spot], info_r.at[spot])
            local = info_in[spot, 0:TOP, 0:NEW] - float(PAIRS[k][p] * XS * ROWS)
            inside = (local >= 0.0) & (local < float(XS * ROWS))
            row = local + jnp.floor(local * (1.0 / ROWS)) * ((GROUP - 1) * ROWS) + float(p * ROWS)
            codes.append(jnp.where(inside, row, -1.0))
            shares.append(info_in[spot, TOP : 2 * TOP, 0:NEW])
        code = jnp.concatenate(codes, axis=1)
        share = jnp.concatenate(shares, axis=1)
        at = lax.broadcasted_iota(jnp.int32, (CROWS, GROUP * NEW), 0).astype(jnp.float32)
        place = jnp.zeros((CROWS, GROUP * NEW), jnp.float32)
        weigh = jnp.zeros((CROWS, GROUP * NEW), jnp.float32)
        for r in range(TOP):
            hit = at == code[r : r + 1, :]
            place = place + jnp.where(hit, 1.0, 0.0)
            weigh = weigh + jnp.where(hit, share[r : r + 1, :], 0.0)
        places[k] = place.astype(jnp.bfloat16)
        high = weigh.astype(jnp.bfloat16)
        share_hi[k] = high
        share_lo[k] = (weigh - high.astype(jnp.float32)).astype(jnp.bfloat16)
        x_go(k, 0)

    def far_routed(k):
        x_go(k, 1)

    def x_go(k, i):
        both = zin[i, GROUP * k : GROUP * (k + 1)].reshape(GROUP * NEW, SLICE)
        xs[i, k] = jnp.dot(places[k], both, preferred_element_type=jnp.float32).astype(
            jnp.bfloat16
        )
        for dx in (1, 3, 2):
            send(
                xs.at[i, k, pl.ds(dx * XROWS, XROWS)],
                rows_in.at[slices[i], pl.ds(k * CROWS + dx * XROWS, XROWS)],
                x_s.at[k, i, dx],
                x_r.at[k, i, dx],
                s,
                at_x(dx),
            )
        rows_in[slices[i], pl.ds(k * CROWS, XROWS), :] = xs[i, k, 0:XROWS, :]

    def y_send(k, i, slice_at, to):
        ref = rows_in.at[slice_at, rows(k)]
        send(ref, ref, y_s.at[k, i], y_r.at[k, i], to, e)

    def y_arrive(k, i, slice_at):
        arrive(rows_in.at[slice_at, rows(k)], y_s.at[k, i], y_r.at[k, i])

    def x_arrive(k, i):
        for dx in (1, 3, 2):
            arrive(
                rows_in.at[slices[i], pl.ds(k * CROWS + dx * XROWS, XROWS)],
                x_s.at[k, i, dx],
                x_r.at[k, i, dx],
            )

    def gather_own(k):
        x_arrive(k, 0)
        y_send(k, 0, s, at_y(1))
        y_send(k, 1, s, at_y(-1))
        y_send(k, 2, s, other)

    def gather_far(k):
        x_arrive(k, 1)
        y_send(k, 3, slices[1], other)

    def gather_next(k):
        y_arrive(k, 0, at_y(-1))
        y_send(k, 4, at_y(-1), other)
        y_arrive(k, 1, at_y(1))
        y_send(k, 5, at_y(1), other)

    def add_slices(k, parity, total):
        def add(dy, total):
            j = lax.rem(y + dy, YS) * 2 + parity
            return total + jnp.dot(
                rows_in[j, rows(k), :], w_in[j], preferred_element_type=jnp.float32
            )

        return lax.fori_loop(0, YS, add, total)

    def early(k):
        if k == 0:
            for copy in loads:
                copy.wait()
        sums[k] = add_slices(k, c, jnp.zeros((CROWS, 2 * UNITS), jnp.float32))

    def compute(k):
        y_arrive(k, 2, other)
        y_arrive(k, 3, pair_y(2))
        y_arrive(k, 4, pair_y(-1))
        y_arrive(k, 5, pair_y(1))
        total = add_slices(k, 1 - c, sums[k])
        gate = total[:, :UNITS]
        hidden = (gate / (1.0 + jnp.exp(-gate)) * total[:, UNITS:]).astype(jnp.bfloat16)

        def down(j):
            part[k, j] = jnp.dot(
                hidden, w_out[j], preferred_element_type=jnp.float32
            ).astype(jnp.bfloat16)

        for dy in (1, 3, 2, 0):
            down(pair_y(dy))
            send(
                part.at[k, pair_y(dy)], sib.at[k, dy], rs_s.at[k, dy], rs_r.at[k, dy], other, e
            )
        for dy in (1, 3, 2, 0):
            down(at_y(dy))

    def plus(a, b):
        return (a.astype(jnp.float32) + b.astype(jnp.float32)).astype(jnp.bfloat16)

    def x_return(k, i):
        for dx in (1, 3, 2):
            send(
                final.at[k, i, pl.ds(dx * XROWS, XROWS)],
                xback.at[i, k, pl.ds(dx * XROWS, XROWS)],
                xb_s.at[k, i, dx],
                xb_r.at[k, i, dx],
                s,
                at_x(-dx),
            )
        xback[i, k, 0:XROWS, :] = final[k, i, 0:XROWS, :]

    def scatter_pair(k):
        for i, dy in ((0, 1), (1, 3)):
            arrive(sib.at[k, dy], rs_s.at[k, dy], rs_r.at[k, dy])
            part[k, at_y(dy)] = plus(part[k, at_y(dy)], sib[k, dy])
            send(
                part.at[k, at_y(dy)],
                whole.at[k, i],
                rs_s.at[k, 4 + i],
                rs_r.at[k, 4 + i],
                at_y(dy),
                e,
            )
        arrive(sib.at[k, 2], rs_s.at[k, 2], rs_r.at[k, 2])
        final[k, 1] = plus(part[k, at_y(2)], sib[k, 2])
        x_return(k, 1)
        arrive(sib.at[k, 0], rs_s.at[k, 0], rs_r.at[k, 0])

    def give_back(k):
        arrive(whole.at[k, 0], rs_s.at[k, 4], rs_r.at[k, 4])
        arrive(whole.at[k, 1], rs_s.at[k, 5], rs_r.at[k, 5])
        final[k, 0] = (
            part[k, s].astype(jnp.float32)
            + sib[k, 0].astype(jnp.float32)
            + whole[k, 0].astype(jnp.float32)
            + whole[k, 1].astype(jnp.float32)
        ).astype(jnp.bfloat16)
        x_return(k, 0)

    def weigh_back(k):
        for i in (1, 0):
            for dx in (1, 3, 2):
                arrive(
                    xback.at[i, k, pl.ds(dx * XROWS, XROWS)],
                    xb_s.at[k, i, dx],
                    xb_r.at[k, i, dx],
                )
            got = xback[i, k]
            over = (((0,), (0,)), ((), ()))
            summed = lax.dot_general(
                share_hi[k], got, over, preferred_element_type=jnp.float32
            ) + lax.dot_general(share_lo[k], got, over, preferred_element_type=jnp.float32)
            zsum[i, GROUP * k : GROUP * (k + 1)] = summed.astype(jnp.bfloat16).reshape(GROUP, NEW, SLICE)
            for p in range(GROUP):
                spot = GROUP * k + p
                if spot:
                    send(
                        zsum.at[i, spot],
                        zback.at[i, spot],
                        zb_s.at[i, spot],
                        zb_r.at[i, spot],
                        s,
                        at_z(-PAIRS[k][p]),
                    )
                else:
                    zback[i, 0] = zsum[i, 0]

    def scores(b, keys, rot_keys):
        over = (((1,), (1,)), ((), ()))
        lat_part = lax.dot_general(
            turned_lat[b * HEADS : (b + 1) * HEADS, :],
            keys,
            over,
            preferred_element_type=jnp.float32,
        )
        half = b % 2
        rot_part = jnp.dot(
            turned_rot[half * HEADS : (half + 1) * HEADS, :],
            rot_keys,
            preferred_element_type=jnp.float32,
        )
        return (lat_part + rot_part) * softmax_scale

    def cached(b):
        if b == 0:
            for n, dy in ((3, 0), (4, -1), (5, 1), (6, 2)):
                key_arrive(n, pair_y(dy))
        here = slice(b * HEADS, (b + 1) * HEADS)
        if b < 2:
            rot_keys = jnp.concatenate([key_rot[...], zero_rot[...]], axis=0)
        else:
            rot_keys = jnp.concatenate([zero_rot[...], key_rot[...]], axis=0)
        older = scores(b, key_lat[...], rot_keys)
        place = lax.broadcasted_iota(jnp.int32, (HEADS, CACHE), 1)
        older = jnp.where(place < prefix[0, 0], older, -jnp.inf)
        high = jnp.max(older, axis=1, keepdims=True)
        weights = jnp.exp(older - high)
        old_high[here, :] = high
        old_total[here, :] = jnp.sum(weights, axis=1, keepdims=True)
        old_sum[here, :] = jnp.dot(
            weights.astype(jnp.bfloat16), key_lat[...], preferred_element_type=jnp.float32
        )

    own, nxt, comp, pair, give, weigh = (
        gather_own,
        gather_next,
        compute,
        scatter_pair,
        give_back,
        weigh_back,
    )
    schedule = (
        (relay, 1),
        (far_relay, 0),
        (routed, 0),
        (queries, 0),
        (relay, 2),
        (far_relay, 1),
        (own, 0),
        (relay, 3),
        (far_routed, 0),
        (routed, 1),
        (queries, 1),
        (far_relay, 2),
        (keys_on, 0),
        (relay, 4),
        (far_relay, 3),
        (gather_far, 0),
        (queries, 2),
        (nxt, 0),
        (own, 1),
        (far_routed, 1),
        (routed, 2),
        (early, 0),
        (far_relay, 4),
        (queries, 3),
        (comp, 0),
        (gather_far, 1),
        (nxt, 1),
        (own, 2),
        (far_routed, 2),
        (routed, 3),
        (early, 1),
        (pair, 0),
        (cached, 0),
        (comp, 1),
        (gather_far, 2),
        (nxt, 2),
        (own, 3),
        (far_routed, 3),
        (early, 2),
        (give, 0),
        (pair, 1),
        (cached, 1),
        (comp, 2),
        (gather_far, 3),
        (nxt, 3),
        (early, 3),
        (weigh, 0),
        (give, 1),
        (pair, 2),
        (cached, 2),
        (comp, 3),
        (weigh, 1),
        (give, 2),
        (pair, 3),
        (cached, 3),
        (weigh, 2),
        (give, 3),
        (weigh, 3),
    )
    for stage, k in schedule:
        stage(k)

    def collect(i):
        total = zback[i, 0].astype(jnp.float32)
        for spot in range(1, ZS):
            arrive(zback.at[i, spot], zb_s.at[i, spot], zb_r.at[i, spot])
            total = total + zback[i, spot].astype(jnp.float32)
        return total

    index = lax.broadcasted_iota(jnp.int32, (NEW, ROPE // 2), 1).astype(jnp.float32)
    position = lax.broadcasted_iota(jnp.int32, (NEW, ROPE // 2), 0) + prefix[0, 0]
    angle = position.astype(jnp.float32) * jnp.exp(index * (-2.0 / ROPE * math.log(rope_base)))
    cosine = jnp.cos(angle)
    sine = jnp.sin(angle)
    far_snd[...] = collect(1).astype(jnp.bfloat16)
    send(far_snd, far_rcv, lat_s.at[0], lat_r.at[0], slices[1], e)
    layer = pick(0) + collect(0)
    arrive(far_rcv, lat_s.at[0], lat_r.at[0])
    layer = (layer + far_rcv[...].astype(jnp.float32)).astype(jnp.bfloat16)
    layer_out[...] = layer
    lat_snd[:, 0:LAT] = jnp.dot(
        layer, w_lat[...], preferred_element_type=jnp.float32
    ).astype(jnp.bfloat16)
    rot = lax.dot_general(
        layer, w_rot[...], (((1,), (1,)), ((), ())), preferred_element_type=jnp.float32
    ).astype(jnp.bfloat16)
    lat_snd[:, LAT:LATPAD] = jnp.concatenate([rot, jnp.zeros_like(rot)], axis=1)
    for j in range(1, SEQ):
        to = lax.rem(s + j, SEQ)
        send(lat_snd, lat_rcv.at[s], lat_s.at[j], lat_r.at[j], to, e)
    for copy in sends[: 1 - SEQ]:
        copy.wait_send()
    raw = lat_snd[...].astype(jnp.float32)
    for j in range(1, SEQ):
        place = lax.rem(s - j + SEQ, SEQ)
        arrive(lat_rcv.at[place], lat_s.at[j], lat_r.at[j])
        raw = raw + lat_rcv[place].astype(jnp.float32)
    fresh = raw[:, 0:LAT]
    fresh_sq = jnp.mean(fresh * fresh, axis=-1, keepdims=True)
    fresh = (fresh * lax.rsqrt(fresh_sq + 1e-06) * latent_gain[...]).astype(jnp.bfloat16)
    first = raw[:, LAT : LAT + ROPE // 2]
    second = raw[:, LAT + ROPE // 2 : LAT + ROPE]
    rotated = jnp.concatenate(
        [first * cosine - second * sine, second * cosine + first * sine], axis=1
    ).T.astype(jnp.bfloat16)
    for b in range(4):
        here = slice(b * HEADS, (b + 1) * HEADS)
        blank = jnp.zeros((ROPE, NEW), jnp.bfloat16)
        both = [rotated, blank] if b < 2 else [blank, rotated]
        newer = scores(b, fresh, jnp.concatenate(both, axis=0))
        place = lax.broadcasted_iota(jnp.int32, (HEADS, NEW), 1)
        asker = lax.broadcasted_iota(jnp.int32, (HEADS, NEW), 0) % 4 + s * 4
        newer = jnp.where(place <= asker, newer, -jnp.inf)
        high = jnp.maximum(old_high[here, :], jnp.max(newer, axis=1, keepdims=True))
        scale = jnp.exp(old_high[here, :] - high)
        weights = jnp.exp(newer - high)
        total = old_total[here, :] * scale + jnp.sum(weights, axis=1, keepdims=True)
        summed = old_sum[here, :] * scale + jnp.dot(
            weights.astype(jnp.bfloat16), fresh, preferred_element_type=jnp.float32
        )
        result = summed * (1.0 / total)
        for i in range(HEADS // 4):
            head = (b % 2 * (HEADS // 4) + i) * 2 + b // 2
            att_out[:, head * LAT : (head + 1) * LAT] = result[4 * i : 4 * i + 4, :].astype(
                jnp.bfloat16
            )
    for copy in sends[1 - SEQ :]:
        copy.wait_send()


def block(*arrays):
    bf = jnp.bfloat16
    f32 = jnp.float32
    dma = pltpu.SemaphoreType.DMA
    vmem = pl.BlockSpec(memory_space=pltpu.VMEM)
    hbm = pl.BlockSpec(memory_space=pl.ANY)
    return pl.pallas_call(
        moe_kernel,
        out_shape=(
            jax.ShapeDtypeStruct((NEW, SLICE), bf),
            jax.ShapeDtypeStruct((4, HEADS * LAT), bf),
        ),
        in_specs=[vmem] * 4
        + [hbm] * 5
        + [vmem, pl.BlockSpec(memory_space=pltpu.SMEM)]
        + [vmem] * 4,
        out_specs=(vmem, vmem),
        scratch_shapes=[
            pltpu.VMEM((TOP, 128), jnp.int32),
            pltpu.VMEM((2 * TOP, 128), f32),
            pltpu.VMEM((ZS, 2 * TOP, 128), f32),
            pltpu.VMEM((SEQ, 16, SLICE), bf),
            pltpu.VMEM((SEQ, 16, SLICE), bf),
            pltpu.VMEM((2, NEW, SLICE), bf),
            pltpu.VMEM((2, ZS, NEW, SLICE), bf),
            pltpu.VMEM((CHUNKS, CROWS, GROUP * NEW), bf),
            pltpu.VMEM((CHUNKS, CROWS, GROUP * NEW), bf),
            pltpu.VMEM((CHUNKS, CROWS, GROUP * NEW), bf),
            pltpu.VMEM((2, CHUNKS, CROWS, SLICE), bf),
            pltpu.VMEM((SEQ, EPS * ROWS, SLICE), bf),
            pltpu.VMEM((SEQ, SLICE, 2 * UNITS), bf),
            pltpu.VMEM((SEQ, UNITS, SLICE), bf),
            pltpu.VMEM((SLICE, 512), bf),
            pltpu.VMEM((64, SLICE), bf),
            pltpu.VMEM((CHUNKS, SEQ, CROWS, SLICE), bf),
            pltpu.VMEM((CHUNKS, CROWS, 2 * UNITS), f32),
            pltpu.VMEM((CHUNKS, YS, CROWS, SLICE), bf),
            pltpu.VMEM((CHUNKS, 2, CROWS, SLICE), bf),
            pltpu.VMEM((CHUNKS, 2, CROWS, SLICE), bf),
            pltpu.VMEM((2, CHUNKS, CROWS, SLICE), bf),
            pltpu.VMEM((2, ZS, NEW, SLICE), bf),
            pltpu.VMEM((2, ZS, NEW, SLICE), bf),
            pltpu.VMEM((NEW, SLICE), bf),
            pltpu.VMEM((NEW, SLICE), bf),
            pltpu.VMEM((NEW, LATPAD), bf),
            pltpu.VMEM((SEQ, NEW, LATPAD), bf),
            pltpu.VMEM((CACHE, LAT), bf),
            pltpu.VMEM((ROPE, CACHE), bf),
            pltpu.VMEM((4 * HEADS, LAT), bf),
            pltpu.VMEM((2 * HEADS, 2 * ROPE), bf),
            pltpu.VMEM((ROPE, CACHE), bf),
            pltpu.VMEM((4 * HEADS, 1), f32),
            pltpu.VMEM((4 * HEADS, 1), f32),
            pltpu.VMEM((4 * HEADS, LAT), f32),
            dma((3 * SEQ + 2,)),
            dma((ZS,)),
            dma((ZS,)),
            dma((SEQ,)),
            dma((SEQ,)),
            dma((2, ZS)),
            dma((2, ZS)),
            dma((CHUNKS, 2, XS)),
            dma((CHUNKS, 2, XS)),
            dma((CHUNKS, 6)),
            dma((CHUNKS, 6)),
            dma((CHUNKS, 6)),
            dma((CHUNKS, 6)),
            dma((CHUNKS, 2, XS)),
            dma((CHUNKS, 2, XS)),
            dma((2, ZS)),
            dma((2, ZS)),
            dma((SEQ,)),
            dma((SEQ,)),
            dma((7, 2)),
            dma((7, 2)),
        ],
        compiler_params=pltpu.CompilerParams(
            collective_id=0, has_side_effects=True, vmem_limit_bytes=56 * 2**20
        ),
        cost_estimate=pl.CostEstimate(
            flops=6_000_000_000, bytes_accessed=14_000_000, transcendentals=131072
        ),
    )(*arrays)


def local(
    entering,
    moe_gain,
    expert_ids,
    gate_weights,
    w_gate,
    w_up,
    w_down,
    w_latent,
    w_rope,
    latent_gain,
    prefix_len,
    cache_latent,
    cache_rope,
    query_latent,
    query_rope,
):
    layer, output = block(
        entering[0],
        moe_gain.reshape(1, -1),
        expert_ids[0].T,
        gate_weights[0].T,
        w_gate[0],
        w_up[0],
        w_down[0],
        w_latent,
        w_rope,
        latent_gain.reshape(1, LAT),
        prefix_len.reshape(1, 1),
        cache_latent[0],
        cache_rope[0],
        query_latent[0],
        query_rope[0],
    )
    return (layer[None], output[None])


def solution(mesh):
    placed = (
        P("ep", "seq", None),
        P(),
        P("ep", None, None),
        P("ep", None, None),
        P("ep", None, "seq"),
        P("ep", None, "seq"),
        P("ep", "seq", None),
        P("seq", None),
        P(None, "seq"),
        P(),
        P("ep"),
        P("ep", "seq", None),
        P("ep", None, "seq"),
        P("ep", "seq", None),
        P("ep", "seq", None),
    )
    return jax.shard_map(
        local,
        mesh=mesh,
        in_specs=placed,
        out_specs=(P("ep", None, "seq"), P("ep", "seq", None)),
        check_vma=False,
    )
```
